1024 devices in a mesh: sx: 64 (over y, x), sy: 16 (over z, core).
Axes of the slice: x: 8, y: 8, z: 8, core: 2. Of those that a mesh axis runs over, the one named last changes fastest.
Arguments:
- strain_rate: float32 [1024, 256, 128], P('sx', 'sy'), may hold values from 0.1 to 10
- deflation: float32 [8, 1024, 256, 128], P(None, 'sx', 'sy'), may hold values from -1.5 to 1.5
- residual: float32 [1024, 256, 128], P('sx', 'sy'), may hold values from -6 to 6
Outputs:
- coarse_blocks: float32 [64, 16, 5, 8, 8], P('sx', 'sy')
- coarse_solution: float32 [64, 16, 8], P('sx', 'sy')
The draws below stay inside these ranges and needn't reach their ends.
All inputs are finite; a program needn't handle non-finite values.
Results may differ from the reference program's by a relative error of at most 0.0003.
Values sent between devices are 32-bit elements; how exact they have to be, the bound alone decides.
No kernel may reach another device: no remote copies, remote signals or barrier semaphores. Data moves between devices by JAX's collectives and lax.ppermute only.
A program may use at most 32 MiB of HBM per device.

```python
import math
import jax
import jax.numpy as jnp
from jax import lax

CX = 16
CY = 16
CZ = 128
NVEC = 8
ITERS = 6
NX = 1024
NY = 256
NZ = 128
N_SX = 64
N_SY = 16


def draw_deflation(key, part):
    along_x = ((jnp.arange(NX) % CX).astype(jnp.float32) * 2.0 + 1.0) / CX - 1.0
    along_y = ((jnp.arange(NY) % CY).astype(jnp.float32) * 2.0 + 1.0) / CY - 1.0
    along_z = ((jnp.arange(NZ) % CZ).astype(jnp.float32) * 2.0 + 1.0) / CZ - 1.0
    shape_all = (NX, NY, NZ)
    coord_x = jnp.broadcast_to(along_x[:, None, None], shape_all)
    coord_y = jnp.broadcast_to(along_y[None, :, None], shape_all)
    coord_z = jnp.broadcast_to(along_z[None, None, :], shape_all)
    constant = jnp.ones(shape_all, jnp.float32)
    basis = jnp.stack([constant, coord_x, coord_y, coord_z, coord_x * coord_y, coord_x * coord_z, coord_y * coord_z, coord_x * coord_y * coord_z])
    rough = jax.random.uniform(key, (NVEC, NX, NY, NZ), jnp.float32, 0.5, 1.5)
    return basis * rough


def level_of(key, shape, cuts, smallest, largest):
    def one(position, parts):
        draws = jax.random.uniform(jax.random.fold_in(jax.random.fold_in(key, 6), position), (parts,), jnp.float32, smallest / len(cuts), largest / len(cuts))
        return jnp.repeat(jnp.exp(draws), shape[position] // parts).reshape((-1,) + (1,) * (len(shape) - position - 1))

    level = one(*cuts[0])
    for cut in cuts[1:]:
        level = level * one(*cut)
    return level


def normal_values(rng, shape, scale, limit, shards=(), kind=jnp.bfloat16):
    array = scale * jax.random.normal(rng, shape, jnp.float32)
    if shards:
        array = array * level_of(rng, shape, shards, -0.22, 0.18)
    return jnp.clip(array, -limit, limit).astype(kind)


def setup_inputs(seed: int = 0) -> dict:
    key_list = jax.random.split(jax.random.key(seed), 4)
    return {
        "strain_rate": jnp.clip(jnp.exp(math.log(10.0) - 4.6051702 * jax.random.uniform(key_list[0], (NX, NY, NZ), jnp.float32) ** level_of(key_list[0], (NX, NY, NZ), ((0, 64), (1, 16)), -0.2, 0.2)), 0.1, 10.0),
        "deflation": draw_deflation(jax.random.fold_in(key_list[3], 71), 0),
        "residual": normal_values(key_list[2], (NX, NY, NZ), 1.0, 6.0, ((0, 64), (1, 16)), jnp.float32),
    }


SIGMA = 0.05
OMEGA = 0.6
HIGH = lax.Precision.HIGHEST

def viscosity(rate):
    return lax.rsqrt(rate) + 0.5 * (1.0 - jnp.exp(-10.0 * rate)) / rate

def block_inverse(self_blocks):
    factor = jnp.linalg.cholesky(self_blocks)
    identity = jnp.broadcast_to(jnp.eye(self_blocks.shape[-1], dtype=self_blocks.dtype), self_blocks.shape)
    lower_inv = jax.scipy.linalg.solve_triangular(factor, identity, lower=True)
    return jnp.einsum('...ka,...kb->...ab', lower_inv, lower_inv, precision=HIGH)

def coarse_update(blocks, inverse, rhs_values, current, lower_row, upper_row, lower_col, upper_col):

    def product_of(index, vector):
        return jnp.einsum('...ab,...b->...a', blocks[..., index, :, :], vector, precision=HIGH)
    remainder = rhs_values - product_of(0, current) - product_of(1, lower_row) - product_of(2, upper_row)
    remainder = remainder - product_of(3, lower_col) - product_of(4, upper_col)
    return current + OMEGA * jnp.einsum('...ab,...b->...a', inverse, remainder, precision=HIGH)

def reference(strain_rate, deflation, residual):
    viscous = viscosity(strain_rate)
    face_x = 0.5 * (viscous[1:] + viscous[:-1])
    face_y = 0.5 * (viscous[:, 1:] + viscous[:, :-1])
    face_z = 0.5 * (viscous[:, :, 1:] + viscous[:, :, :-1])
    wall_x = jnp.concatenate([viscous[:1], face_x, viscous[-1:]], 0)
    wall_y = jnp.concatenate([viscous[:, :1], face_y, viscous[:, -1:]], 1)
    wall_z = jnp.concatenate([viscous[:, :, :1], face_z, viscous[:, :, -1:]], 2)
    diagonal = SIGMA + (wall_x[:-1] + wall_x[1:]) + (wall_y[:, :-1] + wall_y[:, 1:]) + (wall_z[:, :, :-1] + wall_z[:, :, 1:])
    inside_x = ((jnp.arange(NX - 1) + 1) % CX != 0).astype(face_x.dtype)
    inside_y = ((jnp.arange(NY - 1) + 1) % CY != 0).astype(face_y.dtype)
    couple_x = face_x * inside_x[:, None, None]
    couple_y = face_y * inside_y[None, :, None]

    def apply_local(vector):
        nearby = jnp.pad(couple_x * vector[1:], ((0, 1), (0, 0), (0, 0))) + jnp.pad(couple_x * vector[:-1], ((1, 0), (0, 0), (0, 0)))
        nearby = nearby + jnp.pad(couple_y * vector[:, 1:], ((0, 0), (0, 1), (0, 0))) + jnp.pad(couple_y * vector[:, :-1], ((0, 0), (1, 0), (0, 0)))
        nearby = nearby + jnp.pad(face_z * vector[:, :, 1:], ((0, 0), (0, 0), (0, 1))) + jnp.pad(face_z * vector[:, :, :-1], ((0, 0), (0, 0), (1, 0)))
        return diagonal * vector - nearby
    split = deflation.reshape(NVEC, N_SX, CX, N_SY, CY, NZ)

    def self_column(vector):
        image = apply_local(vector).reshape(N_SX, CX, N_SY, CY, NZ)
        return jnp.einsum('aXiYjz,XiYjz->XYa', split, image, precision=HIGH)
    columns = lax.map(self_column, deflation)
    self_blocks = jnp.transpose(columns, (1, 2, 3, 0))
    edge_x = face_x[CX - 1::CX].reshape(N_SX - 1, N_SY, CY, NZ)
    first_x = split[:, :, 0]
    last_x = split[:, :, CX - 1]
    upper_x = -jnp.einsum('aXYjz,XYjz,bXYjz->XYab', last_x[:, :-1], edge_x, first_x[:, 1:], precision=HIGH)
    lower_x = -jnp.einsum('aXYjz,XYjz,bXYjz->XYab', first_x[:, 1:], edge_x, last_x[:, :-1], precision=HIGH)
    zero_x = jnp.zeros((1, N_SY, NVEC, NVEC), upper_x.dtype)
    block_xhi = jnp.concatenate([upper_x, zero_x], 0)
    block_xlo = jnp.concatenate([zero_x, lower_x], 0)
    edge_y = face_y[:, CY - 1::CY].reshape(N_SX, CX, N_SY - 1, NZ)
    first_y = split[:, :, :, :, 0]
    last_y = split[:, :, :, :, CY - 1]
    upper_y = -jnp.einsum('aXiYz,XiYz,bXiYz->XYab', last_y[:, :, :, :-1], edge_y, first_y[:, :, :, 1:], precision=HIGH)
    lower_y = -jnp.einsum('aXiYz,XiYz,bXiYz->XYab', first_y[:, :, :, 1:], edge_y, last_y[:, :, :, :-1], precision=HIGH)
    zero_y = jnp.zeros((N_SX, 1, NVEC, NVEC), upper_y.dtype)
    block_yhi = jnp.concatenate([upper_y, zero_y], 1)
    block_ylo = jnp.concatenate([zero_y, lower_y], 1)
    blocks = jnp.stack([self_blocks, block_xlo, block_xhi, block_ylo, block_yhi], 2)
    rhs_values = jnp.einsum('aXiYjz,XiYjz->XYa', split, residual.reshape(N_SX, CX, N_SY, CY, NZ), precision=HIGH)
    inverse = block_inverse(self_blocks)
    coarse = jnp.zeros((N_SX, N_SY, NVEC), rhs_values.dtype)
    for repeat in range(ITERS):
        lower_row = jnp.pad(coarse[:-1], ((1, 0), (0, 0), (0, 0)))
        upper_row = jnp.pad(coarse[1:], ((0, 1), (0, 0), (0, 0)))
        lower_col = jnp.pad(coarse[:, :-1], ((0, 0), (1, 0), (0, 0)))
        upper_col = jnp.pad(coarse[:, 1:], ((0, 0), (0, 1), (0, 0)))
        coarse = coarse_update(blocks, inverse, rhs_values, coarse, lower_row, upper_row, lower_col, upper_col)
    return (blocks, coarse)
```

```python
import jax
import jax.numpy as jnp
from jax import lax
from jax.experimental import pallas as pl
from jax.experimental.pallas import tpu as pltpu
from jax.sharding import PartitionSpec as P

NVEC = 8
ITERS = 6
SIGMA = 0.05
OMEGA = 0.6
HIGH = lax.Precision.HIGHEST

SELF, XLO, XLO_T, YLO, YLO_T, X_BELOW, Y_BELOW, RHS, WORDS = (0, 64, 128, 192, 256, 320, 384, 448, 512)
WINDOW = 16
PARAMS = pltpu.CompilerParams(vmem_limit_bytes=32 * 1024 * 1024)


def viscosity(rate):
    return lax.rsqrt(rate) + 0.5 * (1.0 - jnp.exp(-10.0 * rate)) / rate


def fold(tiles):
    row = lax.broadcasted_iota(jnp.int32, tiles[0].shape, 0)
    for half in (4, 2, 1):
        low = (row & half) == 0
        count = len(tiles) // 2
        tiles = [
            jnp.where(
                low,
                tiles[i] + pltpu.roll(tiles[i], 8 - half, 0),
                tiles[i + count] + pltpu.roll(tiles[i + count], half, 0),
            )
            for i in range(count)
        ]
    return tiles[0]


def halves(x):
    return x[:8] + x[8:]


def self_kernel(rate_ref, vec_ref, res_ref, out_ref, visc_ref, acc_ref, rhs_ref):
    at_top_x = lax.axis_index("sx") == lax.axis_size("sx") - 1
    at_top_y = lax.axis_index("sy") == lax.axis_size("sy") - 1
    visc_ref[...] = viscosity(rate_ref[...])
    acc_ref[...] = jnp.zeros_like(acc_ref)
    rhs_ref[...] = jnp.zeros_like(rhs_ref)
    cx, cy, cz = rate_ref.shape
    row = lax.broadcasted_iota(jnp.int32, (cy, cz), 0)
    lane = lax.broadcasted_iota(jnp.int32, (cy, cz), 1)
    top_x = jnp.where(at_top_x, 1.0, 0.5)
    top_y = jnp.where(at_top_y, 1.0, 0.5)

    @pl.loop(0, cx)
    def _(i):
        visc = visc_ref[i]
        after = visc_ref[jnp.minimum(i + 1, cx - 1)]
        before = visc_ref[jnp.maximum(i - 1, 0)]
        inner = i < cx - 1
        face_x = jnp.where(inner, 0.5 * (visc + after), 0.0)
        high_x = jnp.where(inner, face_x, top_x * visc)
        low_x = jnp.where(i > 0, 0.5 * (visc + before), 0.5 * visc)
        mean_y = 0.5 * (visc + pltpu.roll(visc, cy - 1, 0))
        face_y = jnp.where(row < cy - 1, mean_y, 0.0)
        high_y = jnp.where(row < cy - 1, mean_y, top_y * visc)
        low_y = jnp.where(row > 0, pltpu.roll(mean_y, 1, 0), 0.5 * visc)
        mean_z = 0.5 * (visc + pltpu.roll(visc, cz - 1, 1))
        face_z = jnp.where(lane < cz - 1, mean_z, 0.0)
        high_z = jnp.where(lane < cz - 1, mean_z, visc)
        low_z = jnp.where(lane > 0, pltpu.roll(mean_z, 1, 1), visc)
        weight = 0.5 * (SIGMA + (low_x + high_x) + (low_y + high_y) + (low_z + high_z))
        res = res_ref[i]
        following = jnp.minimum(i + 1, cx - 1)
        vectors = [vec_ref[a, i] for a in range(NVEC)]
        for a in range(NVEC):
            rhs_ref[a] += halves(vectors[a] * res)
        for b in range(NVEC):
            v = vectors[b]
            image = (
                weight * v
                - face_x * vec_ref[b, following]
                - face_y * pltpu.roll(v, cy - 1, 0)
                - face_z * pltpu.roll(v, cz - 1, 1)
            )
            for a in range(NVEC):
                acc_ref[b * NVEC + a] += halves(vectors[a] * image)

    for b in range(NVEC):
        out_ref[pl.ds(b * NVEC, NVEC), :] = fold(
            [acc_ref[b * NVEC + a] + acc_ref[a * NVEC + b] for a in range(NVEC)]
        )
    out_ref[pl.ds(NVEC * NVEC, NVEC), :] = fold([rhs_ref[a] for a in range(NVEC)])


def face_rows(axis, own, own_rate, below, rows_ref, lo, lo_t, beneath):
    inner = lax.axis_index(axis) > 0
    visc = viscosity(own_rate)
    visc_below = viscosity(jnp.where(inner, below[NVEC], 1.0))
    coupling = jnp.where(inner, -0.5 * (visc + visc_below), 0.0)
    beside = 0.5 * jnp.where(inner, visc_below, visc)
    shared = jnp.where(inner, 0.5 * visc, 0.0)
    first = [own[a] for a in range(NVEC)]
    last = [below[a] for a in range(NVEC)]
    coupled = [coupling * last[b] for b in range(NVEC)]
    cross = [[halves(first[a] * coupled[b]) for a in range(NVEC)] for b in range(NVEC)]
    for b in range(NVEC):
        rows_ref[pl.ds(lo + b * NVEC, NVEC), :] = fold(cross[b])
        rows_ref[pl.ds(lo_t + b * NVEC, NVEC), :] = fold([cross[a][b] for a in range(NVEC)])
    for b in range(NVEC):
        mine = beside * first[b]
        rows_ref[pl.ds(SELF + b * NVEC, NVEC), :] += fold([halves(first[a] * mine) for a in range(NVEC)])
        theirs = shared * last[b]
        rows_ref[pl.ds(beneath + b * NVEC, NVEC), :] = fold([halves(last[a] * theirs) for a in range(NVEC)])


def face_kernel(self_ref, first_x_ref, first_y_ref, below_x_ref, below_y_ref, out_ref, rows_ref):
    rows_ref[pl.ds(SELF, 64), :] = self_ref[pl.ds(0, 64), :]
    rows_ref[pl.ds(RHS, NVEC), :] = self_ref[pl.ds(64, NVEC), :]
    rows_ref[pl.ds(RHS + NVEC, WORDS - RHS - NVEC), :] = jnp.zeros((WORDS - RHS - NVEC, 128), jnp.float32)
    face_rows("sx", first_x_ref, first_x_ref[NVEC], below_x_ref, rows_ref, XLO, XLO_T, X_BELOW)
    face_rows("sy", first_y_ref, first_y_ref[NVEC], below_y_ref, rows_ref, YLO, YLO_T, Y_BELOW)
    message = jnp.sum(rows_ref[...].T, axis=0, keepdims=True)
    out_ref[...] = jnp.broadcast_to(message[None], out_ref.shape)


def solve_kernel(got_ref, blocks_ref, coarse_ref, table_ref):
    count_y, window, words = got_ref.shape
    lanes = count_y * window
    index_x, index_y = lax.axis_index("sx"), lax.axis_index("sy")
    count_x = lax.axis_size("sx")
    place = index_x - window_start(index_x, count_x, window)
    table_ref[...] = got_ref[...].reshape(lanes, words).T
    lane = lax.broadcasted_iota(jnp.int32, (1, lanes), 1)
    has_x = lane % window < window - 1
    has_y = lane < lanes - window

    def columns(base):
        return [table_ref[pl.ds(base + b * NVEC, NVEC), :] for b in range(NVEC)]

    def from_x(value):
        return jnp.where(has_x, pltpu.roll(value, lanes - 1, 1), 0.0)

    def from_y(value):
        return jnp.where(has_y, pltpu.roll(value, lanes - window, 1), 0.0)

    def product(matrix, vector):
        terms = [matrix[b] * vector[b : b + 1] for b in range(NVEC)]
        while len(terms) > 1:
            terms = [terms[i] + terms[i + 1] for i in range(0, len(terms), 2)]
        return terms[0]

    own = [
        s + from_x(x) + from_y(y)
        for s, x, y in zip(columns(SELF), columns(X_BELOW), columns(Y_BELOW))
    ]
    row = lax.broadcasted_iota(jnp.int32, (NVEC, lanes), 0)
    inverse = list(own)
    for k in range(NVEC):
        pivot = 1.0 / inverse[k][k : k + 1]
        at_k = row == k
        column = inverse[k]
        for j in range(NVEC):
            if j != k:
                scaled = inverse[j][k : k + 1] * pivot
                inverse[j] = jnp.where(at_k, scaled, inverse[j] - column * scaled)
        inverse[k] = jnp.where(at_k, pivot, -column * pivot)

    right = table_ref[pl.ds(RHS, NVEC), :]
    xlo, xlo_t, ylo, ylo_t = (columns(base) for base in (XLO, XLO_T, YLO, YLO_T))
    coarse = OMEGA * product(inverse, right)
    for _ in range(ITERS - 1):
        remainder = right - product(own, coarse)
        remainder = remainder - product(xlo, pltpu.roll(coarse, 1, 1)) - from_x(product(xlo_t, coarse))
        remainder = remainder - product(ylo, pltpu.roll(coarse, window, 1)) - from_y(product(ylo_t, coarse))
        coarse = coarse + OMEGA * product(inverse, remainder)
    here = (lane == index_y * window + place).astype(jnp.float32)
    picked = lax.dot_general(
        here, coarse, (((1,), (1,)), ((), ())), precision=HIGH, preferred_element_type=jnp.float32
    )
    coarse_ref[...] = picked

    more_x, more_y = index_x < count_x - 1, index_y < count_y - 1
    mine = got_ref[index_y, pl.ds(place, 1), :]
    next_x = jnp.where(more_x, got_ref[index_y, pl.ds(jnp.minimum(place + 1, window - 1), 1), :], 0.0)
    next_y = jnp.where(more_y, got_ref[jnp.minimum(index_y + 1, count_y - 1), pl.ds(place, 1), :], 0.0)
    flat = [
        mine[:, SELF : SELF + 64] + next_x[:, X_BELOW : X_BELOW + 64] + next_y[:, Y_BELOW : Y_BELOW + 64],
        mine[:, XLO : XLO + 64],
        next_x[:, XLO_T : XLO_T + 64],
        mine[:, YLO : YLO + 64],
        next_y[:, YLO_T : YLO_T + 64],
    ]
    entry = lax.broadcasted_iota(jnp.int32, (NVEC, 64), 1)
    matches = entry % NVEC == lax.broadcasted_iota(jnp.int32, (NVEC, 64), 0)
    spread = jnp.concatenate([jnp.where(matches, f, 0.0) for f in flat], axis=0)
    select = (
        lax.broadcasted_iota(jnp.int32, (64, NVEC), 0) // NVEC == lax.broadcasted_iota(jnp.int32, (64, NVEC), 1)
    ).astype(jnp.float32)
    blocks_ref[...] = jnp.dot(spread, select, precision=HIGH, preferred_element_type=jnp.float32).reshape(5, 8, 8)


def window_start(index, count, window):
    return jnp.clip(index - window // 2, 0, count - window)


def shape(*dims):
    return jax.ShapeDtypeStruct(dims, jnp.float32)


def per_device(strain_rate, deflation, residual):
    count_x, count_y = lax.axis_size("sx"), lax.axis_size("sy")
    index_x = lax.axis_index("sx")
    window = min(WINDOW, count_x)
    last_x = jnp.concatenate([deflation[:, -1], strain_rate[None, -1]], 0)
    last_y = jnp.concatenate([deflation[:, :, -1], strain_rate[None, :, -1]], 0)
    below_x = lax.ppermute(last_x, "sx", [(i, i + 1) for i in range(count_x - 1)])
    below_y = lax.ppermute(last_y, "sy", [(i, i + 1) for i in range(count_y - 1)])
    first_x = jnp.concatenate([deflation[:, 0], strain_rate[None, 0]], 0)
    first_y = jnp.concatenate([deflation[:, :, 0], strain_rate[None, :, 0]], 0)
    cz = strain_rate.shape[-1]
    own_rows = pl.pallas_call(
        self_kernel,
        out_shape=shape(72, cz),
        scratch_shapes=[
            pltpu.VMEM(strain_rate.shape, jnp.float32),
            pltpu.VMEM((64, 8, cz), jnp.float32),
            pltpu.VMEM((NVEC, 8, cz), jnp.float32),
        ],
        compiler_params=PARAMS,
        cost_estimate=pl.CostEstimate(flops=10000000, bytes_accessed=1400000, transcendentals=0),
        name="own_block",
    )(strain_rate, deflation, residual)
    messages = pl.pallas_call(
        face_kernel,
        out_shape=shape(count_x, 1, WORDS),
        scratch_shapes=[pltpu.VMEM((WORDS, cz), jnp.float32)],
        compiler_params=PARAMS,
        name="face_blocks",
    )(own_rows, first_x, first_y, below_x, below_y)
    line = lax.all_to_all(messages, "sx", 0, 0)
    start = window_start(index_x, count_x, window)
    near = lax.dynamic_slice_in_dim(line, start, window, 0).reshape(window, WORDS)
    got = lax.all_to_all(jnp.broadcast_to(near, (count_y, window, WORDS)), "sy", 0, 0)
    blocks, coarse = pl.pallas_call(
        solve_kernel,
        out_shape=(shape(5, NVEC, NVEC), shape(1, NVEC)),
        scratch_shapes=[pltpu.VMEM((WORDS, count_y * window), jnp.float32)],
        compiler_params=PARAMS,
        name="coarse_sweeps",
    )(got)
    return (blocks.reshape(1, 1, 5, NVEC, NVEC), coarse.reshape(1, 1, NVEC))


def solution(mesh):
    placed = (P("sx", "sy", None), P(None, "sx", "sy", None), P("sx", "sy", None))
    return jax.shard_map(
        per_device,
        mesh=mesh,
        in_specs=placed,
        out_specs=(P("sx", "sy", None, None, None), P("sx", "sy", None)),
        check_vma=False,
    )
```

```python
import jax
import jax.numpy as jnp
from jax import lax
from jax.experimental import pallas as pl
from jax.experimental.pallas import tpu as pltpu
from jax.sharding import PartitionSpec as P

NVEC = 8
ITERS = 6
SIGMA = 0.05
OMEGA = 0.6
HIGH = lax.Precision.HIGHEST

PACKED, TRIANGLE, X_DIAG, Y_DIAG, XLO, YLO, RHS, WORDS = (0, 64, 96, 104, 112, 176, 240, 256)
WINDOW = 16
PARAMS = pltpu.CompilerParams(vmem_limit_bytes=32 * 1024 * 1024)


def viscosity(rate):
    return lax.rsqrt(rate) + 0.5 * (1.0 - jnp.exp(-10.0 * rate)) / rate


def fold(tiles):
    row = lax.broadcasted_iota(jnp.int32, tiles[0].shape, 0)
    for half in (4, 2, 1):
        low = (row & half) == 0
        count = len(tiles) // 2
        tiles = [
            jnp.where(
                low,
                tiles[i] + pltpu.roll(tiles[i], 8 - half, 0),
                tiles[i + count] + pltpu.roll(tiles[i + count], half, 0),
            )
            for i in range(count)
        ]
    return tiles[0]


def halves(x):
    return x[:8] + x[8:]


def self_kernel(rate_ref, vec_ref, res_ref, out_ref, visc_ref, acc_ref, rhs_ref):
    at_top_x = lax.axis_index("sx") == lax.axis_size("sx") - 1
    at_top_y = lax.axis_index("sy") == lax.axis_size("sy") - 1
    visc_ref[...] = viscosity(rate_ref[...])
    acc_ref[...] = jnp.zeros_like(acc_ref)
    rhs_ref[...] = jnp.zeros_like(rhs_ref)
    cx, cy, cz = rate_ref.shape
    row = lax.broadcasted_iota(jnp.int32, (cy, cz), 0)
    lane = lax.broadcasted_iota(jnp.int32, (cy, cz), 1)
    top_x = jnp.where(at_top_x, 1.0, 0.5)
    top_y = jnp.where(at_top_y, 1.0, 0.5)

    @pl.loop(0, cx)
    def _(i):
        visc = visc_ref[i]
        after = visc_ref[jnp.minimum(i + 1, cx - 1)]
        before = visc_ref[jnp.maximum(i - 1, 0)]
        inner = i < cx - 1
        face_x = jnp.where(inner, 0.5 * (visc + after), 0.0)
        high_x = jnp.where(inner, face_x, top_x * visc)
        low_x = jnp.where(i > 0, 0.5 * (visc + before), 0.5 * visc)
        mean_y = 0.5 * (visc + pltpu.roll(visc, cy - 1, 0))
        face_y = jnp.where(row < cy - 1, mean_y, 0.0)
        high_y = jnp.where(row < cy - 1, mean_y, top_y * visc)
        low_y = jnp.where(row > 0, pltpu.roll(mean_y, 1, 0), 0.5 * visc)
        mean_z = 0.5 * (visc + pltpu.roll(visc, cz - 1, 1))
        face_z = jnp.where(lane < cz - 1, mean_z, 0.0)
        high_z = jnp.where(lane < cz - 1, mean_z, visc)
        low_z = jnp.where(lane > 0, pltpu.roll(mean_z, 1, 1), visc)
        weight = 0.5 * (SIGMA + (low_x + high_x) + (low_y + high_y) + (low_z + high_z))
        res = res_ref[i]
        following = jnp.minimum(i + 1, cx - 1)
        vectors = [vec_ref[a, i] for a in range(NVEC)]
        for a in range(NVEC):
            rhs_ref[a] += halves(vectors[a] * res)
        for b in range(NVEC):
            v = vectors[b]
            image = (
                weight * v
                - face_x * vec_ref[b, following]
                - face_y * pltpu.roll(v, cy - 1, 0)
                - face_z * pltpu.roll(v, cz - 1, 1)
            )
            for a in range(NVEC):
                acc_ref[b * NVEC + a] += halves(vectors[a] * image)

    for b in range(NVEC):
        out_ref[pl.ds(b * NVEC, NVEC), :] = fold(
            [acc_ref[b * NVEC + a] + acc_ref[a * NVEC + b] for a in range(NVEC)]
        )
    out_ref[pl.ds(NVEC * NVEC, NVEC), :] = fold([rhs_ref[a] for a in range(NVEC)])


def transposed(tiles):
    row = lax.broadcasted_iota(jnp.int32, tiles[0].shape, 0)
    tiles = list(tiles)
    for half in (4, 2, 1):
        low = (row & half) == 0
        for i in range(NVEC):
            if not i & half:
                p, q = tiles[i], tiles[i + half]
                tiles[i] = jnp.where(low, p, pltpu.roll(q, half, 0))
                tiles[i + half] = jnp.where(low, pltpu.roll(p, NVEC - half, 0), q)
    return tiles


def face_columns(axis, own, below):
    inner = lax.axis_index(axis) > 0
    visc = viscosity(own[NVEC])
    visc_below = viscosity(jnp.where(inner, below[NVEC], 1.0))
    coupling = jnp.where(inner, -0.5 * (visc + visc_below), 0.0)
    beside = 0.5 * jnp.where(inner, visc_below, visc)
    shared = jnp.where(inner, 0.5 * visc, 0.0)
    first = [own[a] for a in range(NVEC)]
    last = [below[a] for a in range(NVEC)]

    def gram(left, right, weight):
        columns = []
        for b in range(NVEC):
            scaled = weight * right[b]
            columns.append(fold([halves(left[a] * scaled) for a in range(NVEC)]))
        return columns

    return gram(first, last, coupling), gram(first, first, beside), gram(last, last, shared)


def diagonal_of(columns, row):
    result = columns[0]
    for b in range(1, NVEC):
        result = jnp.where(row == b, columns[b], result)
    return result


def face_kernel(self_ref, first_x_ref, first_y_ref, below_x_ref, below_y_ref, out_ref, rows_ref):
    lo_x, beside_x, beneath_x = face_columns("sx", first_x_ref, below_x_ref)
    lo_y, beside_y, beneath_y = face_columns("sy", first_y_ref, below_y_ref)
    row = lax.broadcasted_iota(jnp.int32, lo_x[0].shape, 0)

    def put(base, value):
        rows_ref[pl.ds(base, NVEC), :] = value

    for b in range(NVEC):
        own = self_ref[pl.ds(b * NVEC, NVEC), :] + beside_x[b] + beside_y[b]
        put(PACKED + b * NVEC, jnp.where(row <= b, own, beneath_x[b]))
        put(XLO + b * NVEC, lo_x[b])
        put(YLO + b * NVEC, lo_y[b])
    for b in range(NVEC // 2):
        far = beneath_y[NVEC - 1 - b]
        put(TRIANGLE + b * NVEC, jnp.where(row > b, beneath_y[b], pltpu.roll(far, b, 0) if b else far))
    put(X_DIAG, diagonal_of(beneath_x, row))
    put(Y_DIAG, diagonal_of(beneath_y, row))
    put(RHS, self_ref[pl.ds(64, NVEC), :])
    put(RHS + NVEC, jnp.zeros_like(lo_x[0]))
    message = jnp.sum(rows_ref[...].T, axis=0, keepdims=True)
    out_ref[...] = jnp.broadcast_to(message[None], out_ref.shape)


def solve_kernel(got_ref, blocks_ref, coarse_ref, table_ref):
    count_y, window, words = got_ref.shape
    lanes = count_y * window
    index_x, index_y = lax.axis_index("sx"), lax.axis_index("sy")
    count_x = lax.axis_size("sx")
    place = index_x - window_start(index_x, count_x, window)
    table_ref[...] = got_ref[...].reshape(lanes, words).T
    lane = lax.broadcasted_iota(jnp.int32, (1, lanes), 1)
    row = lax.broadcasted_iota(jnp.int32, (NVEC, lanes), 0)
    has_x = lane % window < window - 1
    has_y = lane < lanes - window

    def columns(base, count=NVEC):
        return [table_ref[pl.ds(base + b * NVEC, NVEC), :] for b in range(count)]

    def from_x(value):
        return jnp.where(has_x, pltpu.roll(value, lanes - 1, 1), 0.0)

    def from_y(value):
        return jnp.where(has_y, pltpu.roll(value, lanes - window, 1), 0.0)

    def product(matrix, vector):
        terms = [matrix[b] * vector[b : b + 1] for b in range(NVEC)]
        while len(terms) > 1:
            terms = [terms[i] + terms[i + 1] for i in range(0, len(terms), 2)]
        return terms[0]

    def mirrored(lower, upper, diagonal):
        return [
            jnp.where(row > b, lower[b], jnp.where(row < b, upper[b], diagonal)) for b in range(NVEC)
        ]

    packed = columns(PACKED)
    packed_t = transposed(packed)
    x_diag, y_diag = columns(X_DIAG, 2)
    beneath_x = mirrored(packed, packed_t, x_diag)
    lower = columns(TRIANGLE, NVEC // 2)
    lower = lower + [pltpu.roll(lower[c], NVEC - c, 0) if c else lower[c] for c in (3, 2, 1, 0)]
    beneath_y = mirrored(lower, transposed(lower), y_diag)
    own = [
        jnp.where(row <= b, packed[b], packed_t[b]) + from_x(beneath_x[b]) + from_y(beneath_y[b])
        for b in range(NVEC)
    ]
    inverse = list(own)
    for k in range(NVEC):
        pivot = 1.0 / inverse[k][k : k + 1]
        at_k = row == k
        column = inverse[k]
        for j in range(NVEC):
            if j != k:
                scaled = inverse[j][k : k + 1] * pivot
                inverse[j] = jnp.where(at_k, scaled, inverse[j] - column * scaled)
        inverse[k] = jnp.where(at_k, pivot, -column * pivot)

    right = table_ref[pl.ds(RHS, NVEC), :]
    xlo, ylo = columns(XLO), columns(YLO)
    xlo_t, ylo_t = transposed(xlo), transposed(ylo)
    coarse = OMEGA * product(inverse, right)
    for _ in range(ITERS - 1):
        remainder = right - product(own, coarse)
        remainder = remainder - product(xlo, pltpu.roll(coarse, 1, 1)) - from_x(product(xlo_t, coarse))
        remainder = remainder - product(ylo, pltpu.roll(coarse, window, 1)) - from_y(product(ylo_t, coarse))
        coarse = coarse + OMEGA * product(inverse, remainder)

    here = (lane == index_y * window + place).astype(jnp.float32)
    results = jnp.concatenate(
        own + xlo + [from_x(m) for m in xlo_t] + ylo + [from_y(m) for m in ylo_t] + [coarse], axis=0
    )
    flat = lax.dot_general(
        jnp.broadcast_to(here, (NVEC, lanes)),
        results,
        (((1,), (1,)), ((), ())),
        precision=HIGH,
        preferred_element_type=jnp.float32,
    )
    coarse_ref[...] = flat[:1, 320:328]
    entry = lax.broadcasted_iota(jnp.int32, (NVEC, 64), 1)
    matches = entry % NVEC == lax.broadcasted_iota(jnp.int32, (NVEC, 64), 0)
    spread = jnp.concatenate(
        [jnp.where(matches, flat[:, s * 64 : s * 64 + 64], 0.0) for s in range(5)], axis=0
    )
    select = (
        lax.broadcasted_iota(jnp.int32, (64, NVEC), 0) // NVEC == lax.broadcasted_iota(jnp.int32, (64, NVEC), 1)
    ).astype(jnp.float32)
    blocks_ref[...] = jnp.dot(spread, select, precision=HIGH, preferred_element_type=jnp.float32).reshape(5, 8, 8)


def window_start(index, count, window):
    return jnp.clip(index - window // 2, 0, count - window)


def shape(*dims):
    return jax.ShapeDtypeStruct(dims, jnp.float32)


def per_device(strain_rate, deflation, residual):
    count_x, count_y = lax.axis_size("sx"), lax.axis_size("sy")
    index_x = lax.axis_index("sx")
    window = min(WINDOW, count_x)
    last_x = jnp.concatenate([deflation[:, -1], strain_rate[None, -1]], 0)
    last_y = jnp.concatenate([deflation[:, :, -1], strain_rate[None, :, -1]], 0)
    below_x = lax.ppermute(last_x, "sx", [(i, i + 1) for i in range(count_x - 1)])
    below_y = lax.ppermute(last_y, "sy", [(i, i + 1) for i in range(count_y - 1)])
    first_x = jnp.concatenate([deflation[:, 0], strain_rate[None, 0]], 0)
    first_y = jnp.concatenate([deflation[:, :, 0], strain_rate[None, :, 0]], 0)
    cz = strain_rate.shape[-1]
    own_rows = pl.pallas_call(
        self_kernel,
        out_shape=shape(72, cz),
        scratch_shapes=[
            pltpu.VMEM(strain_rate.shape, jnp.float32),
            pltpu.VMEM((64, 8, cz), jnp.float32),
            pltpu.VMEM((NVEC, 8, cz), jnp.float32),
        ],
        compiler_params=PARAMS,
        cost_estimate=pl.CostEstimate(flops=10000000, bytes_accessed=1400000, transcendentals=0),
        name="own_block",
    )(strain_rate, deflation, residual)
    messages = pl.pallas_call(
        face_kernel,
        out_shape=shape(count_x, 1, WORDS),
        scratch_shapes=[pltpu.VMEM((WORDS, cz), jnp.float32)],
        compiler_params=PARAMS,
        name="face_blocks",
    )(own_rows, first_x, first_y, below_x, below_y)
    line = lax.all_to_all(messages, "sx", 0, 0)
    start = window_start(index_x, count_x, window)
    near = lax.dynamic_slice_in_dim(line, start, window, 0).reshape(window, WORDS)
    got = lax.all_to_all(jnp.broadcast_to(near, (count_y, window, WORDS)), "sy", 0, 0)
    blocks, coarse = pl.pallas_call(
        solve_kernel,
        out_shape=(shape(5, NVEC, NVEC), shape(1, NVEC)),
        scratch_shapes=[pltpu.VMEM((WORDS, count_y * window), jnp.float32)],
        compiler_params=PARAMS,
        name="coarse_sweeps",
    )(got)
    return (blocks.reshape(1, 1, 5, NVEC, NVEC), coarse.reshape(1, 1, NVEC))


def solution(mesh):
    placed = (P("sx", "sy", None), P(None, "sx", "sy", None), P("sx", "sy", None))
    return jax.shard_map(
        per_device,
        mesh=mesh,
        in_specs=placed,
        out_specs=(P("sx", "sy", None, None, None), P("sx", "sy", None)),
        check_vma=False,
    )
```

```python
import jax
import jax.numpy as jnp
from jax import lax
from jax.experimental import pallas as pl
from jax.experimental.pallas import tpu as pltpu
from jax.sharding import PartitionSpec as P

NVEC = 8
ITERS = 6
SIGMA = 0.05
OMEGA = 0.6
HIGH = lax.Precision.HIGHEST

PACKED, TRIANGLE, X_DIAG, Y_DIAG, XLO, YLO, RHS, WORDS = (0, 64, 96, 104, 112, 176, 240, 256)
WINDOW = 16
ROW = 8
PARAMS = pltpu.CompilerParams(vmem_limit_bytes=32 * 1024 * 1024)


def viscosity(rate):
    return lax.rsqrt(rate) + 0.5 * (1.0 - jnp.exp(-10.0 * rate)) / rate


def fold(tiles):
    row = lax.broadcasted_iota(jnp.int32, tiles[0].shape, 0)
    for half in (4, 2, 1):
        low = (row & half) == 0
        count = len(tiles) // 2
        tiles = [
            jnp.where(
                low,
                tiles[i] + pltpu.roll(tiles[i], 8 - half, 0),
                tiles[i + count] + pltpu.roll(tiles[i + count], half, 0),
            )
            for i in range(count)
        ]
    return tiles[0]


def halves(x):
    return x[:8] + x[8:]


def self_kernel(rate_ref, vec_ref, res_ref, out_ref, visc_ref, acc_ref, rhs_ref):
    at_top_x = lax.axis_index("sx") == lax.axis_size("sx") - 1
    at_top_y = lax.axis_index("sy") == lax.axis_size("sy") - 1
    visc_ref[...] = viscosity(rate_ref[...])
    acc_ref[...] = jnp.zeros_like(acc_ref)
    rhs_ref[...] = jnp.zeros_like(rhs_ref)
    cx, cy, cz = rate_ref.shape
    row = lax.broadcasted_iota(jnp.int32, (cy, cz), 0)
    lane = lax.broadcasted_iota(jnp.int32, (cy, cz), 1)
    top_x = jnp.where(at_top_x, 1.0, 0.5)
    top_y = jnp.where(at_top_y, 1.0, 0.5)

    @pl.loop(0, cx)
    def _(i):
        visc = visc_ref[i]
        after = visc_ref[jnp.minimum(i + 1, cx - 1)]
        before = visc_ref[jnp.maximum(i - 1, 0)]
        inner = i < cx - 1
        face_x = jnp.where(inner, 0.5 * (visc + after), 0.0)
        high_x = jnp.where(inner, face_x, top_x * visc)
        low_x = jnp.where(i > 0, 0.5 * (visc + before), 0.5 * visc)
        mean_y = 0.5 * (visc + pltpu.roll(visc, cy - 1, 0))
        face_y = jnp.where(row < cy - 1, mean_y, 0.0)
        high_y = jnp.where(row < cy - 1, mean_y, top_y * visc)
        low_y = jnp.where(row > 0, pltpu.roll(mean_y, 1, 0), 0.5 * visc)
        mean_z = 0.5 * (visc + pltpu.roll(visc, cz - 1, 1))
        face_z = jnp.where(lane < cz - 1, mean_z, 0.0)
        high_z = jnp.where(lane < cz - 1, mean_z, visc)
        low_z = jnp.where(lane > 0, pltpu.roll(mean_z, 1, 1), visc)
        weight = 0.5 * (SIGMA + (low_x + high_x) + (low_y + high_y) + (low_z + high_z))
        res = res_ref[i]
        following = jnp.minimum(i + 1, cx - 1)
        vectors = [vec_ref[a, i] for a in range(NVEC)]
        for a in range(NVEC):
            rhs_ref[a] += halves(vectors[a] * res)
        for b in range(NVEC):
            v = vectors[b]
            image = (
                weight * v
                - face_x * vec_ref[b, following]
                - face_y * pltpu.roll(v, cy - 1, 0)
                - face_z * pltpu.roll(v, cz - 1, 1)
            )
            for a in range(NVEC):
                acc_ref[b * NVEC + a] += halves(vectors[a] * image)

    for b in range(NVEC):
        out_ref[pl.ds(b * NVEC, NVEC), :] = fold(
            [acc_ref[b * NVEC + a] + acc_ref[a * NVEC + b] for a in range(NVEC)]
        )
    out_ref[pl.ds(NVEC * NVEC, NVEC), :] = fold([rhs_ref[a] for a in range(NVEC)])


def transposed(tiles):
    row = lax.broadcasted_iota(jnp.int32, tiles[0].shape, 0)
    tiles = list(tiles)
    for half in (4, 2, 1):
        low = (row & half) == 0
        for i in range(NVEC):
            if not i & half:
                p, q = tiles[i], tiles[i + half]
                tiles[i] = jnp.where(low, p, pltpu.roll(q, half, 0))
                tiles[i + half] = jnp.where(low, pltpu.roll(p, NVEC - half, 0), q)
    return tiles


def face_columns(axis, own, below):
    inner = lax.axis_index(axis) > 0
    visc = viscosity(own[NVEC])
    visc_below = viscosity(jnp.where(inner, below[NVEC], 1.0))
    coupling = jnp.where(inner, -0.5 * (visc + visc_below), 0.0)
    beside = 0.5 * jnp.where(inner, visc_below, visc)
    shared = jnp.where(inner, 0.5 * visc, 0.0)
    first = [own[a] for a in range(NVEC)]
    last = [below[a] for a in range(NVEC)]

    def gram(left, right, weight):
        columns = []
        for b in range(NVEC):
            scaled = weight * right[b]
            columns.append(fold([halves(left[a] * scaled) for a in range(NVEC)]))
        return columns

    return gram(first, last, coupling), gram(first, first, beside), gram(last, last, shared)


def diagonal_of(columns, row):
    result = columns[0]
    for b in range(1, NVEC):
        result = jnp.where(row == b, columns[b], result)
    return result


def face_kernel(self_ref, first_x_ref, first_y_ref, below_x_ref, below_y_ref, out_ref, rows_ref):
    lo_x, beside_x, beneath_x = face_columns("sx", first_x_ref, below_x_ref)
    lo_y, beside_y, beneath_y = face_columns("sy", first_y_ref, below_y_ref)
    row = lax.broadcasted_iota(jnp.int32, lo_x[0].shape, 0)

    def put(base, value):
        rows_ref[pl.ds(base, NVEC), :] = value

    for b in range(NVEC):
        own = self_ref[pl.ds(b * NVEC, NVEC), :] + beside_x[b] + beside_y[b]
        put(PACKED + b * NVEC, jnp.where(row <= b, own, beneath_x[b]))
        put(XLO + b * NVEC, lo_x[b])
        put(YLO + b * NVEC, lo_y[b])
    for b in range(NVEC // 2):
        far = beneath_y[NVEC - 1 - b]
        put(TRIANGLE + b * NVEC, jnp.where(row > b, beneath_y[b], pltpu.roll(far, b, 0) if b else far))
    put(X_DIAG, diagonal_of(beneath_x, row))
    put(Y_DIAG, diagonal_of(beneath_y, row))
    put(RHS, self_ref[pl.ds(64, NVEC), :])
    put(RHS + NVEC, jnp.zeros_like(lo_x[0]))
    message = jnp.sum(rows_ref[...].T, axis=0, keepdims=True)
    out_ref[...] = jnp.broadcast_to(message[None], out_ref.shape)


def solve_kernel(got_ref, blocks_ref, coarse_ref, table_ref):
    count_y, window, words = got_ref.shape
    lanes = count_y * window
    index_x, index_y = lax.axis_index("sx"), lax.axis_index("sy")
    place = ROW + index_x % ROW - window_start(index_x, lax.axis_size("sx"))
    table_ref[...] = got_ref[...].reshape(lanes, words).T
    lane = lax.broadcasted_iota(jnp.int32, (1, lanes), 1)
    row = lax.broadcasted_iota(jnp.int32, (NVEC, lanes), 0)
    has_x = lane % window < window - 1
    has_y = lane < lanes - window

    def columns(base, count=NVEC):
        return [table_ref[pl.ds(base + b * NVEC, NVEC), :] for b in range(count)]

    def from_x(value):
        return jnp.where(has_x, pltpu.roll(value, lanes - 1, 1), 0.0)

    def from_y(value):
        return jnp.where(has_y, pltpu.roll(value, lanes - window, 1), 0.0)

    def product(matrix, vector):
        terms = [matrix[b] * vector[b : b + 1] for b in range(NVEC)]
        while len(terms) > 1:
            terms = [terms[i] + terms[i + 1] for i in range(0, len(terms), 2)]
        return terms[0]

    def mirrored(lower, upper, diagonal):
        return [
            jnp.where(row > b, lower[b], jnp.where(row < b, upper[b], diagonal)) for b in range(NVEC)
        ]

    packed = columns(PACKED)
    packed_t = transposed(packed)
    x_diag, y_diag = columns(X_DIAG, 2)
    beneath_x = mirrored(packed, packed_t, x_diag)
    lower = columns(TRIANGLE, NVEC // 2)
    lower = lower + [pltpu.roll(lower[c], NVEC - c, 0) if c else lower[c] for c in (3, 2, 1, 0)]
    beneath_y = mirrored(lower, transposed(lower), y_diag)
    own = [
        jnp.where(row <= b, packed[b], packed_t[b]) + from_x(beneath_x[b]) + from_y(beneath_y[b])
        for b in range(NVEC)
    ]
    inverse = list(own)
    for k in range(NVEC):
        pivot = 1.0 / inverse[k][k : k + 1]
        at_k = row == k
        column = inverse[k]
        for j in range(NVEC):
            if j != k:
                scaled = inverse[j][k : k + 1] * pivot
                inverse[j] = jnp.where(at_k, scaled, inverse[j] - column * scaled)
        inverse[k] = jnp.where(at_k, pivot, -column * pivot)

    right = table_ref[pl.ds(RHS, NVEC), :]
    xlo, ylo = columns(XLO), columns(YLO)
    xlo_t, ylo_t = transposed(xlo), transposed(ylo)
    coarse = OMEGA * product(inverse, right)
    for _ in range(ITERS - 1):
        remainder = right - product(own, coarse)
        remainder = remainder - product(xlo, pltpu.roll(coarse, 1, 1)) - from_x(product(xlo_t, coarse))
        remainder = remainder - product(ylo, pltpu.roll(coarse, window, 1)) - from_y(product(ylo_t, coarse))
        coarse = coarse + OMEGA * product(inverse, remainder)

    here = (lane == index_y * window + place).astype(jnp.float32)
    results = jnp.concatenate(
        own + xlo + [from_x(m) for m in xlo_t] + ylo + [from_y(m) for m in ylo_t] + [coarse], axis=0
    )
    flat = lax.dot_general(
        jnp.broadcast_to(here, (NVEC, lanes)),
        results,
        (((1,), (1,)), ((), ())),
        precision=HIGH,
        preferred_element_type=jnp.float32,
    )
    coarse_ref[...] = flat[:1, 320:328]
    entry = lax.broadcasted_iota(jnp.int32, (NVEC, 64), 1)
    matches = entry % NVEC == lax.broadcasted_iota(jnp.int32, (NVEC, 64), 0)
    spread = jnp.concatenate(
        [jnp.where(matches, flat[:, s * 64 : s * 64 + 64], 0.0) for s in range(5)], axis=0
    )
    select = (
        lax.broadcasted_iota(jnp.int32, (64, NVEC), 0) // NVEC == lax.broadcasted_iota(jnp.int32, (64, NVEC), 1)
    ).astype(jnp.float32)
    blocks_ref[...] = jnp.dot(spread, select, precision=HIGH, preferred_element_type=jnp.float32).reshape(5, 8, 8)


def window_start(index, count):
    chip_row = index // ROW
    low = jnp.where(chip_row > 0, 0, ROW)
    high = jnp.where(chip_row < count // ROW - 1, 3 * ROW, 2 * ROW) - WINDOW
    return jnp.clip(ROW + index % ROW - WINDOW // 2, low, high)


def window_kernel(lower_ref, line_ref, upper_ref, out_ref, rows_ref, near_ref):
    start = window_start(lax.axis_index("sx"), lax.axis_size("sx"))
    for part, ref in enumerate((lower_ref, line_ref, upper_ref)):
        for i in range(ROW):
            rows_ref[pl.ds(part * ROW + i, 1), :] = ref[i]
    for i in range(WINDOW):
        near_ref[pl.ds(i, 1), :] = rows_ref[pl.ds(start + i, 1), :]
    out_ref[...] = jnp.broadcast_to(near_ref[...][None], out_ref.shape)


def shape(*dims):
    return jax.ShapeDtypeStruct(dims, jnp.float32)


def per_device(strain_rate, deflation, residual):
    count_x, count_y = lax.axis_size("sx"), lax.axis_size("sy")
    last_x = jnp.concatenate([deflation[:, -1], strain_rate[None, -1]], 0)
    last_y = jnp.concatenate([deflation[:, :, -1], strain_rate[None, :, -1]], 0)
    below_x = lax.ppermute(last_x, "sx", [(i, i + 1) for i in range(count_x - 1)])
    below_y = lax.ppermute(last_y, "sy", [(i, i + 1) for i in range(count_y - 1)])
    first_x = jnp.concatenate([deflation[:, 0], strain_rate[None, 0]], 0)
    first_y = jnp.concatenate([deflation[:, :, 0], strain_rate[None, :, 0]], 0)
    cz = strain_rate.shape[-1]
    own_rows = pl.pallas_call(
        self_kernel,
        out_shape=shape(72, cz),
        scratch_shapes=[
            pltpu.VMEM(strain_rate.shape, jnp.float32),
            pltpu.VMEM((64, 8, cz), jnp.float32),
            pltpu.VMEM((NVEC, 8, cz), jnp.float32),
        ],
        compiler_params=PARAMS,
        cost_estimate=pl.CostEstimate(flops=10000000, bytes_accessed=1400000, transcendentals=0),
        name="own_block",
    )(strain_rate, deflation, residual)
    messages = pl.pallas_call(
        face_kernel,
        out_shape=shape(ROW, 1, WORDS),
        scratch_shapes=[pltpu.VMEM((WORDS, cz), jnp.float32)],
        compiler_params=PARAMS,
        name="face_blocks",
    )(own_rows, first_x, first_y, below_x, below_y)
    rows = [[ROW * g + i for i in range(ROW)] for g in range(count_x // ROW)]
    line = lax.all_to_all(messages, "sx", 0, 0, axis_index_groups=rows)
    lower = lax.ppermute(line, "sx", [(i, i + ROW) for i in range(count_x - ROW)])
    upper = lax.ppermute(line, "sx", [(i + ROW, i) for i in range(count_x - ROW)])
    near = pl.pallas_call(
        window_kernel,
        out_shape=shape(count_y, WINDOW, WORDS),
        scratch_shapes=[pltpu.VMEM((3 * ROW, WORDS), jnp.float32), pltpu.VMEM((WINDOW, WORDS), jnp.float32)],
        compiler_params=PARAMS,
        name="window",
    )(lower, line, upper)
    got = lax.all_to_all(near, "sy", 0, 0)
    blocks, coarse = pl.pallas_call(
        solve_kernel,
        out_shape=(shape(5, NVEC, NVEC), shape(1, NVEC)),
        scratch_shapes=[pltpu.VMEM((WORDS, count_y * WINDOW), jnp.float32)],
        compiler_params=PARAMS,
        name="coarse_sweeps",
    )(got)
    return (blocks.reshape(1, 1, 5, NVEC, NVEC), coarse.reshape(1, 1, NVEC))


def solution(mesh):
    placed = (P("sx", "sy", None), P(None, "sx", "sy", None), P("sx", "sy", None))
    return jax.shard_map(
        per_device,
        mesh=mesh,
        in_specs=placed,
        out_specs=(P("sx", "sy", None, None, None), P("sx", "sy", None)),
        check_vma=False,
    )
```

```python
import jax
import jax.numpy as jnp
from jax import lax
from jax.experimental import pallas as pl
from jax.experimental.pallas import tpu as pltpu
from jax.sharding import PartitionSpec as P

NVEC = 8
ITERS = 6
SIGMA = 0.05
OMEGA = 0.6
HIGH = lax.Precision.HIGHEST

PACKED, TRIANGLE, X_DIAG, Y_DIAG, XLO, YLO, RHS, WORDS = (0, 64, 96, 104, 112, 176, 240, 256)
WINDOW = 16
ROW = 8
CORES = 2
REACH = 3
LINES = 2 * CORES * (REACH + 1)
PARAMS = pltpu.CompilerParams(vmem_limit_bytes=32 * 1024 * 1024)


def viscosity(rate):
    return lax.rsqrt(rate) + 0.5 * (1.0 - jnp.exp(-10.0 * rate)) / rate


def fold(tiles):
    row = lax.broadcasted_iota(jnp.int32, tiles[0].shape, 0)
    for half in (4, 2, 1):
        low = (row & half) == 0
        count = len(tiles) // 2
        tiles = [
            jnp.where(
                low,
                tiles[i] + pltpu.roll(tiles[i], 8 - half, 0),
                tiles[i + count] + pltpu.roll(tiles[i + count], half, 0),
            )
            for i in range(count)
        ]
    return tiles[0]


def halves(x):
    return x[:8] + x[8:]


def self_kernel(rate_ref, vec_ref, res_ref, out_ref, visc_ref, acc_ref, rhs_ref):
    at_top_x = lax.axis_index("sx") == lax.axis_size("sx") - 1
    at_top_y = lax.axis_index("sy") == lax.axis_size("sy") - 1
    visc_ref[...] = viscosity(rate_ref[...])
    acc_ref[...] = jnp.zeros_like(acc_ref)
    rhs_ref[...] = jnp.zeros_like(rhs_ref)
    cx, cy, cz = rate_ref.shape
    row = lax.broadcasted_iota(jnp.int32, (cy, cz), 0)
    lane = lax.broadcasted_iota(jnp.int32, (cy, cz), 1)
    top_x = jnp.where(at_top_x, 1.0, 0.5)
    top_y = jnp.where(at_top_y, 1.0, 0.5)

    @pl.loop(0, cx)
    def _(i):
        visc = visc_ref[i]
        after = visc_ref[jnp.minimum(i + 1, cx - 1)]
        before = visc_ref[jnp.maximum(i - 1, 0)]
        inner = i < cx - 1
        face_x = jnp.where(inner, 0.5 * (visc + after), 0.0)
        high_x = jnp.where(inner, face_x, top_x * visc)
        low_x = jnp.where(i > 0, 0.5 * (visc + before), 0.5 * visc)
        mean_y = 0.5 * (visc + pltpu.roll(visc, cy - 1, 0))
        face_y = jnp.where(row < cy - 1, mean_y, 0.0)
        high_y = jnp.where(row < cy - 1, mean_y, top_y * visc)
        low_y = jnp.where(row > 0, pltpu.roll(mean_y, 1, 0), 0.5 * visc)
        mean_z = 0.5 * (visc + pltpu.roll(visc, cz - 1, 1))
        face_z = jnp.where(lane < cz - 1, mean_z, 0.0)
        high_z = jnp.where(lane < cz - 1, mean_z, visc)
        low_z = jnp.where(lane > 0, pltpu.roll(mean_z, 1, 1), visc)
        weight = 0.5 * (SIGMA + (low_x + high_x) + (low_y + high_y) + (low_z + high_z))
        res = res_ref[i]
        following = jnp.minimum(i + 1, cx - 1)
        vectors = [vec_ref[a, i] for a in range(NVEC)]
        for a in range(NVEC):
            rhs_ref[a] += halves(vectors[a] * res)
        for b in range(NVEC):
            v = vectors[b]
            image = (
                weight * v
                - face_x * vec_ref[b, following]
                - face_y * pltpu.roll(v, cy - 1, 0)
                - face_z * pltpu.roll(v, cz - 1, 1)
            )
            for a in range(NVEC):
                acc_ref[b * NVEC + a] += halves(vectors[a] * image)

    for b in range(NVEC):
        out_ref[pl.ds(b * NVEC, NVEC), :] = fold(
            [acc_ref[b * NVEC + a] + acc_ref[a * NVEC + b] for a in range(NVEC)]
        )
    out_ref[pl.ds(NVEC * NVEC, NVEC), :] = fold([rhs_ref[a] for a in range(NVEC)])


def transposed(tiles):
    row = lax.broadcasted_iota(jnp.int32, tiles[0].shape, 0)
    tiles = list(tiles)
    for half in (4, 2, 1):
        low = (row & half) == 0
        for i in range(NVEC):
            if not i & half:
                p, q = tiles[i], tiles[i + half]
                tiles[i] = jnp.where(low, p, pltpu.roll(q, half, 0))
                tiles[i + half] = jnp.where(low, pltpu.roll(p, NVEC - half, 0), q)
    return tiles


def face_columns(axis, own, below):
    inner = lax.axis_index(axis) > 0
    visc = viscosity(own[NVEC])
    visc_below = viscosity(jnp.where(inner, below[NVEC], 1.0))
    coupling = jnp.where(inner, -0.5 * (visc + visc_below), 0.0)
    beside = 0.5 * jnp.where(inner, visc_below, visc)
    shared = jnp.where(inner, 0.5 * visc, 0.0)
    first = [own[a] for a in range(NVEC)]
    last = [below[a] for a in range(NVEC)]

    def gram(left, right, weight):
        columns = []
        for b in range(NVEC):
            scaled = weight * right[b]
            columns.append(fold([halves(left[a] * scaled) for a in range(NVEC)]))
        return columns

    return gram(first, last, coupling), gram(first, first, beside), gram(last, last, shared)


def diagonal_of(columns, row):
    result = columns[0]
    for b in range(1, NVEC):
        result = jnp.where(row == b, columns[b], result)
    return result


def face_kernel(self_ref, first_x_ref, first_y_ref, below_x_ref, below_y_ref, out_ref, rows_ref):
    lo_x, beside_x, beneath_x = face_columns("sx", first_x_ref, below_x_ref)
    lo_y, beside_y, beneath_y = face_columns("sy", first_y_ref, below_y_ref)
    row = lax.broadcasted_iota(jnp.int32, lo_x[0].shape, 0)

    def put(base, value):
        rows_ref[pl.ds(base, NVEC), :] = value

    for b in range(NVEC):
        own = self_ref[pl.ds(b * NVEC, NVEC), :] + beside_x[b] + beside_y[b]
        put(PACKED + b * NVEC, jnp.where(row <= b, own, beneath_x[b]))
        put(XLO + b * NVEC, lo_x[b])
        put(YLO + b * NVEC, lo_y[b])
    for b in range(NVEC // 2):
        far = beneath_y[NVEC - 1 - b]
        put(TRIANGLE + b * NVEC, jnp.where(row > b, beneath_y[b], pltpu.roll(far, b, 0) if b else far))
    put(X_DIAG, diagonal_of(beneath_x, row))
    put(Y_DIAG, diagonal_of(beneath_y, row))
    put(RHS, self_ref[pl.ds(64, NVEC), :])
    put(RHS + NVEC, jnp.zeros_like(lo_x[0]))
    message = jnp.sum(rows_ref[...].T, axis=0, keepdims=True)
    out_ref[...] = jnp.broadcast_to(message[None], out_ref.shape)


def solve_kernel(near_ref, mine_ref, other_ref, blocks_ref, coarse_ref, table_ref):
    window, words = near_ref.shape[1:]
    lanes = LINES * window
    index_x, index_y = lax.axis_index("sx"), lax.axis_index("sy")
    core, chip = index_y % CORES, index_y // CORES
    place = ROW + index_x % ROW - window_start(index_x, lax.axis_size("sx"))
    below = [jnp.where(core == 0, mine_ref[i], other_ref[i]) for i in range(CORES * REACH)]
    above = [jnp.where(core == 0, other_ref[i], mine_ref[i]) for i in range(CORES * REACH)]
    parts = [jnp.zeros((CORES * window, words), jnp.float32)]
    for step in range(REACH, 0, -1):
        parts += below[CORES * (step - 1) : CORES * step]
    parts += [near_ref[i] for i in range(CORES)] + above
    table_ref[...] = jnp.concatenate(parts, axis=0).T
    lane = lax.broadcasted_iota(jnp.int32, (1, lanes), 1)
    row = lax.broadcasted_iota(jnp.int32, (NVEC, lanes), 0)
    away = lane // (CORES * window) - (REACH + 1)
    count_chips = lax.axis_size("sy") // CORES
    filled = (away >= -REACH) & (chip + away >= 0) & (chip + away < count_chips)
    unit = jnp.where(filled, 0.0, 1.0)
    has_x = lane % window < window - 1
    has_y = lane < lanes - window

    def columns(base, count=NVEC):
        return [table_ref[pl.ds(base + b * NVEC, NVEC), :] for b in range(count)]

    def from_x(value):
        return jnp.where(has_x, pltpu.roll(value, lanes - 1, 1), 0.0)

    def from_y(value):
        return jnp.where(has_y, pltpu.roll(value, lanes - window, 1), 0.0)

    def product(matrix, vector):
        terms = [matrix[b] * vector[b : b + 1] for b in range(NVEC)]
        while len(terms) > 1:
            terms = [terms[i] + terms[i + 1] for i in range(0, len(terms), 2)]
        return terms[0]

    def mirrored(lower, upper, diagonal):
        return [
            jnp.where(row > b, lower[b], jnp.where(row < b, upper[b], diagonal)) for b in range(NVEC)
        ]

    packed = columns(PACKED)
    packed_t = transposed(packed)
    x_diag, y_diag = columns(X_DIAG, 2)
    beneath_x = mirrored(packed, packed_t, x_diag)
    lower = columns(TRIANGLE, NVEC // 2)
    lower = lower + [pltpu.roll(lower[c], NVEC - c, 0) if c else lower[c] for c in (3, 2, 1, 0)]
    beneath_y = mirrored(lower, transposed(lower), y_diag)
    own = [
        jnp.where(row <= b, packed[b], packed_t[b])
        + from_x(beneath_x[b])
        + from_y(beneath_y[b])
        + jnp.where(row == b, unit, 0.0)
        for b in range(NVEC)
    ]
    inverse = list(own)
    for k in range(NVEC):
        pivot = 1.0 / inverse[k][k : k + 1]
        at_k = row == k
        column = inverse[k]
        for j in range(NVEC):
            if j != k:
                scaled = inverse[j][k : k + 1] * pivot
                inverse[j] = jnp.where(at_k, scaled, inverse[j] - column * scaled)
        inverse[k] = jnp.where(at_k, pivot, -column * pivot)

    right = table_ref[pl.ds(RHS, NVEC), :]
    xlo, ylo = columns(XLO), columns(YLO)
    xlo_t, ylo_t = transposed(xlo), transposed(ylo)
    coarse = OMEGA * product(inverse, right)
    for _ in range(ITERS - 1):
        remainder = right - product(own, coarse)
        remainder = remainder - product(xlo, pltpu.roll(coarse, 1, 1)) - from_x(product(xlo_t, coarse))
        remainder = remainder - product(ylo, pltpu.roll(coarse, window, 1)) - from_y(product(ylo_t, coarse))
        coarse = coarse + OMEGA * product(inverse, remainder)

    here = (lane == (CORES * (REACH + 1) + core) * window + place).astype(jnp.float32)
    results = jnp.concatenate(
        own + xlo + [from_x(m) for m in xlo_t] + ylo + [from_y(m) for m in ylo_t] + [coarse], axis=0
    )
    flat = lax.dot_general(
        jnp.broadcast_to(here, (NVEC, lanes)),
        results,
        (((1,), (1,)), ((), ())),
        precision=HIGH,
        preferred_element_type=jnp.float32,
    )
    coarse_ref[...] = flat[:1, 320:328]
    entry = lax.broadcasted_iota(jnp.int32, (NVEC, 64), 1)
    matches = entry % NVEC == lax.broadcasted_iota(jnp.int32, (NVEC, 64), 0)
    spread = jnp.concatenate(
        [jnp.where(matches, flat[:, s * 64 : s * 64 + 64], 0.0) for s in range(5)], axis=0
    )
    select = (
        lax.broadcasted_iota(jnp.int32, (64, NVEC), 0) // NVEC == lax.broadcasted_iota(jnp.int32, (64, NVEC), 1)
    ).astype(jnp.float32)
    blocks_ref[...] = jnp.dot(spread, select, precision=HIGH, preferred_element_type=jnp.float32).reshape(5, 8, 8)


def window_start(index, count):
    chip_row = index // ROW
    low = jnp.where(chip_row > 0, 0, ROW)
    high = jnp.where(chip_row < count // ROW - 1, 3 * ROW, 2 * ROW) - WINDOW
    return jnp.clip(ROW + index % ROW - WINDOW // 2, low, high)


def window_kernel(lower_ref, line_ref, upper_ref, out_ref, rows_ref):
    start = window_start(lax.axis_index("sx"), lax.axis_size("sx"))
    count = CORES * ROW
    for part, ref in enumerate((lower_ref, line_ref, upper_ref)):
        for i in range(count):
            rows_ref[pl.ds(part * count + i, 1), :] = ref[i]
    for core in range(CORES):
        for i in range(WINDOW):
            out_ref[core, pl.ds(i, 1), :] = rows_ref[pl.ds(CORES * (start + i) + core, 1), :]


def shape(*dims):
    return jax.ShapeDtypeStruct(dims, jnp.float32)


def per_device(strain_rate, deflation, residual):
    count_x, count_y = lax.axis_size("sx"), lax.axis_size("sy")
    last_x = jnp.concatenate([deflation[:, -1], strain_rate[None, -1]], 0)
    last_y = jnp.concatenate([deflation[:, :, -1], strain_rate[None, :, -1]], 0)
    below_x = lax.ppermute(last_x, "sx", [(i, i + 1) for i in range(count_x - 1)])
    below_y = lax.ppermute(last_y, "sy", [(i, i + 1) for i in range(count_y - 1)])
    first_x = jnp.concatenate([deflation[:, 0], strain_rate[None, 0]], 0)
    first_y = jnp.concatenate([deflation[:, :, 0], strain_rate[None, :, 0]], 0)
    cz = strain_rate.shape[-1]
    own_rows = pl.pallas_call(
        self_kernel,
        out_shape=shape(72, cz),
        scratch_shapes=[
            pltpu.VMEM(strain_rate.shape, jnp.float32),
            pltpu.VMEM((64, 8, cz), jnp.float32),
            pltpu.VMEM((NVEC, 8, cz), jnp.float32),
        ],
        compiler_params=PARAMS,
        cost_estimate=pl.CostEstimate(flops=10000000, bytes_accessed=1400000, transcendentals=0),
        name="own_block",
    )(strain_rate, deflation, residual)
    messages = pl.pallas_call(
        face_kernel,
        out_shape=shape(CORES * ROW, 1, WORDS),
        scratch_shapes=[pltpu.VMEM((WORDS, cz), jnp.float32)],
        compiler_params=PARAMS,
        name="face_blocks",
    )(own_rows, first_x, first_y, below_x, below_y)
    chips = range(count_y // CORES)
    rows = [
        [(ROW * g + i) * count_y + CORES * z + c for i in range(ROW) for c in range(CORES)]
        for g in range(count_x // ROW)
        for z in chips
    ]
    line = lax.all_to_all(messages, ("sx", "sy"), 0, 0, axis_index_groups=rows)
    lower = lax.ppermute(line, "sx", [(i, i + ROW) for i in range(count_x - ROW)])
    upper = lax.ppermute(line, "sx", [(i + ROW, i) for i in range(count_x - ROW)])
    near = pl.pallas_call(
        window_kernel,
        out_shape=shape(CORES, WINDOW, WORDS),
        scratch_shapes=[pltpu.VMEM((3 * CORES * ROW, WORDS), jnp.float32)],
        compiler_params=PARAMS,
        name="window",
    )(lower, line, upper)
    received = []
    for step in range(1, REACH + 1):
        up = [(CORES * z, CORES * (z + step)) for z in chips if z + step in chips]
        down = [(CORES * z + 1, CORES * (z - step) + 1) for z in chips if z - step in chips]
        received.append(lax.ppermute(near, "sy", up + down))
    mine = jnp.concatenate(received, axis=0)
    swap = [(CORES * z + c, CORES * z + 1 - c) for z in chips for c in range(CORES)]
    other = lax.ppermute(mine, "sy", swap)
    blocks, coarse = pl.pallas_call(
        solve_kernel,
        out_shape=(shape(5, NVEC, NVEC), shape(1, NVEC)),
        scratch_shapes=[pltpu.VMEM((WORDS, LINES * WINDOW), jnp.float32)],
        compiler_params=PARAMS,
        name="coarse_sweeps",
    )(near, mine, other)
    return (blocks.reshape(1, 1, 5, NVEC, NVEC), coarse.reshape(1, 1, NVEC))


def solution(mesh):
    placed = (P("sx", "sy", None), P(None, "sx", "sy", None), P("sx", "sy", None))
    return jax.shard_map(
        per_device,
        mesh=mesh,
        in_specs=placed,
        out_specs=(P("sx", "sy", None, None, None), P("sx", "sy", None)),
        check_vma=False,
    )
```

```python
import jax
import jax.numpy as jnp
from jax import lax
from jax.experimental import pallas as pl
from jax.experimental.pallas import tpu as pltpu
from jax.sharding import PartitionSpec as P

NVEC = 8
ITERS = 6
SIGMA = 0.05
OMEGA = 0.6
HIGH = lax.Precision.HIGHEST

PACKED, TRIANGLE, X_DIAG, Y_DIAG, XLO, YLO, RHS, WORDS = (0, 64, 96, 104, 112, 176, 240, 256)
WINDOW = 16
ROW = 8
PARAMS = pltpu.CompilerParams(vmem_limit_bytes=32 * 1024 * 1024)


def viscosity(rate):
    return lax.rsqrt(rate) + 0.5 * (1.0 - jnp.exp(-10.0 * rate)) / rate


def fold(tiles):
    row = lax.broadcasted_iota(jnp.int32, tiles[0].shape, 0)
    for half in (4, 2, 1):
        low = (row & half) == 0
        count = len(tiles) // 2
        tiles = [
            jnp.where(
                low,
                tiles[i] + pltpu.roll(tiles[i], 8 - half, 0),
                tiles[i + count] + pltpu.roll(tiles[i + count], half, 0),
            )
            for i in range(count)
        ]
    return tiles[0]


def halves(x):
    return x[:8] + x[8:]


def self_kernel(rate_ref, vec_ref, res_ref, out_ref, visc_ref, acc_ref, rhs_ref):
    at_top_x = lax.axis_index("sx") == lax.axis_size("sx") - 1
    at_top_y = lax.axis_index("sy") == lax.axis_size("sy") - 1
    visc_ref[...] = viscosity(rate_ref[...])
    acc_ref[...] = jnp.zeros_like(acc_ref)
    rhs_ref[...] = jnp.zeros_like(rhs_ref)
    cx, cy, cz = rate_ref.shape
    row = lax.broadcasted_iota(jnp.int32, (cy, cz), 0)
    lane = lax.broadcasted_iota(jnp.int32, (cy, cz), 1)
    top_x = jnp.where(at_top_x, 1.0, 0.5)
    top_y = jnp.where(at_top_y, 1.0, 0.5)

    @pl.loop(0, cx)
    def _(i):
        visc = visc_ref[i]
        after = visc_ref[jnp.minimum(i + 1, cx - 1)]
        before = visc_ref[jnp.maximum(i - 1, 0)]
        inner = i < cx - 1
        face_x = jnp.where(inner, 0.5 * (visc + after), 0.0)
        high_x = jnp.where(inner, face_x, top_x * visc)
        low_x = jnp.where(i > 0, 0.5 * (visc + before), 0.5 * visc)
        mean_y = 0.5 * (visc + pltpu.roll(visc, cy - 1, 0))
        face_y = jnp.where(row < cy - 1, mean_y, 0.0)
        high_y = jnp.where(row < cy - 1, mean_y, top_y * visc)
        low_y = jnp.where(row > 0, pltpu.roll(mean_y, 1, 0), 0.5 * visc)
        mean_z = 0.5 * (visc + pltpu.roll(visc, cz - 1, 1))
        face_z = jnp.where(lane < cz - 1, mean_z, 0.0)
        high_z = jnp.where(lane < cz - 1, mean_z, visc)
        low_z = jnp.where(lane > 0, pltpu.roll(mean_z, 1, 1), visc)
        weight = 0.5 * (SIGMA + (low_x + high_x) + (low_y + high_y) + (low_z + high_z))
        res = res_ref[i]
        following = jnp.minimum(i + 1, cx - 1)
        vectors = [vec_ref[a, i] for a in range(NVEC)]
        for a in range(NVEC):
            rhs_ref[a] += halves(vectors[a] * res)
        for b in range(NVEC):
            v = vectors[b]
            image = (
                weight * v
                - face_x * vec_ref[b, following]
                - face_y * pltpu.roll(v, cy - 1, 0)
                - face_z * pltpu.roll(v, cz - 1, 1)
            )
            for a in range(NVEC):
                acc_ref[b * NVEC + a] += halves(vectors[a] * image)

    for b in range(NVEC):
        out_ref[pl.ds(b * NVEC, NVEC), :] = fold(
            [acc_ref[b * NVEC + a] + acc_ref[a * NVEC + b] for a in range(NVEC)]
        )
    out_ref[pl.ds(NVEC * NVEC, NVEC), :] = fold([rhs_ref[a] for a in range(NVEC)])


def transposed(tiles):
    row = lax.broadcasted_iota(jnp.int32, tiles[0].shape, 0)
    tiles = list(tiles)
    for half in (4, 2, 1):
        low = (row & half) == 0
        for i in range(NVEC):
            if not i & half:
                p, q = tiles[i], tiles[i + half]
                tiles[i] = jnp.where(low, p, pltpu.roll(q, half, 0))
                tiles[i + half] = jnp.where(low, pltpu.roll(p, NVEC - half, 0), q)
    return tiles


def face_columns(axis, own, below):
    inner = lax.axis_index(axis) > 0
    visc = viscosity(own[NVEC])
    visc_below = viscosity(jnp.where(inner, below[NVEC], 1.0))
    coupling = jnp.where(inner, -0.5 * (visc + visc_below), 0.0)
    beside = 0.5 * jnp.where(inner, visc_below, visc)
    shared = jnp.where(inner, 0.5 * visc, 0.0)
    first = [own[a] for a in range(NVEC)]
    last = [below[a] for a in range(NVEC)]

    def gram(left, right, weight):
        columns = []
        for b in range(NVEC):
            scaled = weight * right[b]
            columns.append(fold([halves(left[a] * scaled) for a in range(NVEC)]))
        return columns

    return gram(first, last, coupling), gram(first, first, beside), gram(last, last, shared)


def diagonal_of(columns, row):
    result = columns[0]
    for b in range(1, NVEC):
        result = jnp.where(row == b, columns[b], result)
    return result


def face_kernel(self_ref, first_x_ref, first_y_ref, below_x_ref, below_y_ref, out_ref, rows_ref):
    lo_x, beside_x, beneath_x = face_columns("sx", first_x_ref, below_x_ref)
    lo_y, beside_y, beneath_y = face_columns("sy", first_y_ref, below_y_ref)
    row = lax.broadcasted_iota(jnp.int32, lo_x[0].shape, 0)

    def put(base, value):
        rows_ref[pl.ds(base, NVEC), :] = value

    for b in range(NVEC):
        own = self_ref[pl.ds(b * NVEC, NVEC), :] + beside_x[b] + beside_y[b]
        put(PACKED + b * NVEC, jnp.where(row <= b, own, beneath_x[b]))
        put(XLO + b * NVEC, lo_x[b])
        put(YLO + b * NVEC, lo_y[b])
    for b in range(NVEC // 2):
        far = beneath_y[NVEC - 1 - b]
        put(TRIANGLE + b * NVEC, jnp.where(row > b, beneath_y[b], pltpu.roll(far, b, 0) if b else far))
    put(X_DIAG, diagonal_of(beneath_x, row))
    put(Y_DIAG, diagonal_of(beneath_y, row))
    put(RHS, self_ref[pl.ds(64, NVEC), :])
    put(RHS + NVEC, jnp.zeros_like(lo_x[0]))
    message = jnp.sum(rows_ref[...].T, axis=0, keepdims=True)
    out_ref[...] = jnp.broadcast_to(message[None], out_ref.shape)


def solve_kernel(lower_ref, line_ref, upper_ref, blocks_ref, coarse_ref, rows_ref, table_ref):
    count_y, words = line_ref.shape[1:]
    lanes = WINDOW * count_y
    index_x, index_y = lax.axis_index("sx"), lax.axis_index("sy")
    start = window_start(index_x, lax.axis_size("sx"))
    place = ROW + index_x % ROW - start
    for part, ref in enumerate((lower_ref, line_ref, upper_ref)):
        rows_ref[pl.ds(part * ROW, ROW)] = ref[...]
    table_ref[...] = rows_ref[pl.ds(start, WINDOW)].reshape(lanes, words).T
    lane = lax.broadcasted_iota(jnp.int32, (1, lanes), 1)
    row = lax.broadcasted_iota(jnp.int32, (NVEC, lanes), 0)
    has_x = lane < lanes - count_y
    has_y = lane % count_y < count_y - 1

    def columns(base, count=NVEC):
        return [table_ref[pl.ds(base + b * NVEC, NVEC), :] for b in range(count)]

    def from_x(value):
        return jnp.where(has_x, pltpu.roll(value, lanes - count_y, 1), 0.0)

    def from_y(value):
        return jnp.where(has_y, pltpu.roll(value, lanes - 1, 1), 0.0)

    def product(matrix, vector):
        terms = [matrix[b] * vector[b : b + 1] for b in range(NVEC)]
        while len(terms) > 1:
            terms = [terms[i] + terms[i + 1] for i in range(0, len(terms), 2)]
        return terms[0]

    def mirrored(lower, upper, diagonal):
        return [
            jnp.where(row > b, lower[b], jnp.where(row < b, upper[b], diagonal)) for b in range(NVEC)
        ]

    packed = columns(PACKED)
    packed_t = transposed(packed)
    x_diag, y_diag = columns(X_DIAG, 2)
    beneath_x = mirrored(packed, packed_t, x_diag)
    lower = columns(TRIANGLE, NVEC // 2)
    lower = lower + [pltpu.roll(lower[c], NVEC - c, 0) if c else lower[c] for c in (3, 2, 1, 0)]
    beneath_y = mirrored(lower, transposed(lower), y_diag)
    own = [
        jnp.where(row <= b, packed[b], packed_t[b]) + from_x(beneath_x[b]) + from_y(beneath_y[b])
        for b in range(NVEC)
    ]
    inverse = list(own)
    for k in range(NVEC):
        pivot = 1.0 / inverse[k][k : k + 1]
        at_k = row == k
        column = inverse[k]
        for j in range(NVEC):
            if j != k:
                scaled = inverse[j][k : k + 1] * pivot
                inverse[j] = jnp.where(at_k, scaled, inverse[j] - column * scaled)
        inverse[k] = jnp.where(at_k, pivot, -column * pivot)

    right = table_ref[pl.ds(RHS, NVEC), :]
    xlo, ylo = columns(XLO), columns(YLO)
    xlo_t, ylo_t = transposed(xlo), transposed(ylo)
    coarse = OMEGA * product(inverse, right)
    for _ in range(ITERS - 1):
        remainder = right - product(own, coarse)
        remainder = remainder - product(xlo, pltpu.roll(coarse, count_y, 1)) - from_x(product(xlo_t, coarse))
        remainder = remainder - product(ylo, pltpu.roll(coarse, 1, 1)) - from_y(product(ylo_t, coarse))
        coarse = coarse + OMEGA * product(inverse, remainder)

    here = (lane == place * count_y + index_y).astype(jnp.float32)
    results = jnp.concatenate(
        own + xlo + [from_x(m) for m in xlo_t] + ylo + [from_y(m) for m in ylo_t] + [coarse], axis=0
    )
    flat = lax.dot_general(
        jnp.broadcast_to(here, (NVEC, lanes)),
        results,
        (((1,), (1,)), ((), ())),
        precision=HIGH,
        preferred_element_type=jnp.float32,
    )
    coarse_ref[...] = flat[:1, 320:328]
    entry = lax.broadcasted_iota(jnp.int32, (NVEC, 64), 1)
    matches = entry % NVEC == lax.broadcasted_iota(jnp.int32, (NVEC, 64), 0)
    spread = jnp.concatenate(
        [jnp.where(matches, flat[:, s * 64 : s * 64 + 64], 0.0) for s in range(5)], axis=0
    )
    select = (
        lax.broadcasted_iota(jnp.int32, (64, NVEC), 0) // NVEC == lax.broadcasted_iota(jnp.int32, (64, NVEC), 1)
    ).astype(jnp.float32)
    blocks_ref[...] = jnp.dot(spread, select, precision=HIGH, preferred_element_type=jnp.float32).reshape(5, 8, 8)


def window_start(index, count):
    chip_row = index // ROW
    low = jnp.where(chip_row > 0, 0, ROW)
    high = jnp.where(chip_row < count // ROW - 1, 3 * ROW, 2 * ROW) - WINDOW
    return jnp.clip(ROW + index % ROW - WINDOW // 2, low, high)


def shape(*dims):
    return jax.ShapeDtypeStruct(dims, jnp.float32)


def per_device(strain_rate, deflation, residual):
    count_x, count_y = lax.axis_size("sx"), lax.axis_size("sy")
    last_x = jnp.concatenate([deflation[:, -1], strain_rate[None, -1]], 0)
    last_y = jnp.concatenate([deflation[:, :, -1], strain_rate[None, :, -1]], 0)
    below_x = lax.ppermute(last_x, "sx", [(i, i + 1) for i in range(count_x - 1)])
    below_y = lax.ppermute(last_y, "sy", [(i, i + 1) for i in range(count_y - 1)])
    first_x = jnp.concatenate([deflation[:, 0], strain_rate[None, 0]], 0)
    first_y = jnp.concatenate([deflation[:, :, 0], strain_rate[None, :, 0]], 0)
    cz = strain_rate.shape[-1]
    own_rows = pl.pallas_call(
        self_kernel,
        out_shape=shape(72, cz),
        scratch_shapes=[
            pltpu.VMEM(strain_rate.shape, jnp.float32),
            pltpu.VMEM((64, 8, cz), jnp.float32),
            pltpu.VMEM((NVEC, 8, cz), jnp.float32),
        ],
        compiler_params=PARAMS,
        cost_estimate=pl.CostEstimate(flops=10000000, bytes_accessed=1400000, transcendentals=0),
        name="own_block",
    )(strain_rate, deflation, residual)
    messages = pl.pallas_call(
        face_kernel,
        out_shape=shape(count_y, 1, WORDS),
        scratch_shapes=[pltpu.VMEM((WORDS, cz), jnp.float32)],
        compiler_params=PARAMS,
        name="face_blocks",
    )(own_rows, first_x, first_y, below_x, below_y)
    across = lax.all_to_all(messages, "sy", 0, 0).reshape(count_y, WORDS)
    rows = [[ROW * g + i for i in range(ROW)] for g in range(count_x // ROW)]
    line = lax.all_to_all(
        jnp.broadcast_to(across, (ROW, count_y, WORDS)), "sx", 0, 0, axis_index_groups=rows
    )
    lower = lax.ppermute(line, "sx", [(i, i + ROW) for i in range(count_x - ROW)])
    upper = lax.ppermute(line, "sx", [(i + ROW, i) for i in range(count_x - ROW)])
    blocks, coarse = pl.pallas_call(
        solve_kernel,
        out_shape=(shape(5, NVEC, NVEC), shape(1, NVEC)),
        scratch_shapes=[
            pltpu.VMEM((3 * ROW, count_y, WORDS), jnp.float32),
            pltpu.VMEM((WORDS, count_y * WINDOW), jnp.float32),
        ],
        compiler_params=PARAMS,
        name="coarse_sweeps",
    )(lower, line, upper)
    return (blocks.reshape(1, 1, 5, NVEC, NVEC), coarse.reshape(1, 1, NVEC))


def solution(mesh):
    placed = (P("sx", "sy", None), P(None, "sx", "sy", None), P("sx", "sy", None))
    return jax.shard_map(
        per_device,
        mesh=mesh,
        in_specs=placed,
        out_specs=(P("sx", "sy", None, None, None), P("sx", "sy", None)),
        check_vma=False,
    )
```

```python
import jax
import jax.numpy as jnp
from jax import lax
from jax.experimental import pallas as pl
from jax.experimental.pallas import tpu as pltpu
from jax.sharding import PartitionSpec as P

NVEC = 8
ITERS = 6
SIGMA = 0.05
OMEGA = 0.6
HIGH = lax.Precision.HIGHEST

PACKED, TRIANGLE, X_DIAG, Y_DIAG, XLO, YLO, RHS, WORDS = (0, 64, 96, 104, 112, 176, 240, 256)
WINDOW = 16
CHUNK = 4
CHUNKS = 4
ROW = 8
PARAMS = pltpu.CompilerParams(vmem_limit_bytes=32 * 1024 * 1024)


def viscosity(rate):
    return lax.rsqrt(rate) + 0.5 * (1.0 - jnp.exp(-10.0 * rate)) / rate


def fold(tiles):
    row = lax.broadcasted_iota(jnp.int32, tiles[0].shape, 0)
    for half in (4, 2, 1):
        low = (row & half) == 0
        count = len(tiles) // 2
        tiles = [
            jnp.where(
                low,
                tiles[i] + pltpu.roll(tiles[i], 8 - half, 0),
                tiles[i + count] + pltpu.roll(tiles[i + count], half, 0),
            )
            for i in range(count)
        ]
    return tiles[0]


def halves(x):
    return x[:8] + x[8:]


def self_kernel(rate_ref, far_ref, res_ref, out_ref, vec_ref, visc_ref, acc_ref, rhs_ref, sems):
    copies = []
    for k in range(CHUNKS):
        part = (slice(None), pl.ds(k * CHUNK, CHUNK))
        copies.append(pltpu.make_async_copy(far_ref.at[part], vec_ref.at[part], sems.at[k]))
        copies[k].start()
    at_top_x = lax.axis_index("sx") == lax.axis_size("sx") - 1
    at_top_y = lax.axis_index("sy") == lax.axis_size("sy") - 1
    visc_ref[...] = viscosity(rate_ref[...])
    acc_ref[...] = jnp.zeros_like(acc_ref)
    rhs_ref[...] = jnp.zeros_like(rhs_ref)
    cx, cy, cz = rate_ref.shape
    row = lax.broadcasted_iota(jnp.int32, (cy, cz), 0)
    lane = lax.broadcasted_iota(jnp.int32, (cy, cz), 1)
    top_x = jnp.where(at_top_x, 1.0, 0.5)
    top_y = jnp.where(at_top_y, 1.0, 0.5)

    def layer(i):
        visc = visc_ref[i]
        after = visc_ref[jnp.minimum(i + 1, cx - 1)]
        before = visc_ref[jnp.maximum(i - 1, 0)]
        inner = i < cx - 1
        face_x = jnp.where(inner, 0.5 * (visc + after), 0.0)
        high_x = jnp.where(inner, face_x, top_x * visc)
        low_x = jnp.where(i > 0, 0.5 * (visc + before), 0.5 * visc)
        mean_y = 0.5 * (visc + pltpu.roll(visc, cy - 1, 0))
        face_y = jnp.where(row < cy - 1, mean_y, 0.0)
        high_y = jnp.where(row < cy - 1, mean_y, top_y * visc)
        low_y = jnp.where(row > 0, pltpu.roll(mean_y, 1, 0), 0.5 * visc)
        mean_z = 0.5 * (visc + pltpu.roll(visc, cz - 1, 1))
        face_z = jnp.where(lane < cz - 1, mean_z, 0.0)
        high_z = jnp.where(lane < cz - 1, mean_z, visc)
        low_z = jnp.where(lane > 0, pltpu.roll(mean_z, 1, 1), visc)
        weight = 0.5 * (SIGMA + (low_x + high_x) + (low_y + high_y) + (low_z + high_z))
        res = res_ref[i]
        following = jnp.minimum(i + 1, cx - 1)
        vectors = [vec_ref[a, i] for a in range(NVEC)]
        for a in range(NVEC):
            rhs_ref[a] += halves(vectors[a] * res)
        for b in range(NVEC):
            v = vectors[b]
            image = (
                weight * v
                - face_x * vec_ref[b, following]
                - face_y * pltpu.roll(v, cy - 1, 0)
                - face_z * pltpu.roll(v, cz - 1, 1)
            )
            for a in range(NVEC):
                acc_ref[b * NVEC + a] += halves(vectors[a] * image)

    copies[0].wait()
    for k in range(CHUNKS):
        if k + 1 < CHUNKS:
            copies[k + 1].wait()
        pl.loop(k * CHUNK, (k + 1) * CHUNK, unroll=2)(layer)

    for b in range(NVEC):
        out_ref[pl.ds(b * NVEC, NVEC), :] = fold(
            [acc_ref[b * NVEC + a] + acc_ref[a * NVEC + b] for a in range(NVEC)]
        )
    out_ref[pl.ds(NVEC * NVEC, NVEC), :] = fold([rhs_ref[a] for a in range(NVEC)])


def transposed(tiles):
    row = lax.broadcasted_iota(jnp.int32, tiles[0].shape, 0)
    tiles = list(tiles)
    for half in (4, 2, 1):
        low = (row & half) == 0
        for i in range(NVEC):
            if not i & half:
                p, q = tiles[i], tiles[i + half]
                tiles[i] = jnp.where(low, p, pltpu.roll(q, half, 0))
                tiles[i + half] = jnp.where(low, pltpu.roll(p, NVEC - half, 0), q)
    return tiles


def face_columns(axis, own, below):
    inner = lax.axis_index(axis) > 0
    visc = viscosity(own[NVEC])
    visc_below = viscosity(jnp.where(inner, below[NVEC], 1.0))
    coupling = jnp.where(inner, -0.5 * (visc + visc_below), 0.0)
    beside = 0.5 * jnp.where(inner, visc_below, visc)
    shared = jnp.where(inner, 0.5 * visc, 0.0)
    first = [own[a] for a in range(NVEC)]
    last = [below[a] for a in range(NVEC)]

    def gram(left, right, weight):
        columns = []
        for b in range(NVEC):
            scaled = weight * right[b]
            columns.append(fold([halves(left[a] * scaled) for a in range(NVEC)]))
        return columns

    return gram(first, last, coupling), gram(first, first, beside), gram(last, last, shared)


def diagonal_of(columns, row):
    result = columns[0]
    for b in range(1, NVEC):
        result = jnp.where(row == b, columns[b], result)
    return result


def face_kernel(self_ref, first_x_ref, first_y_ref, below_x_ref, below_y_ref, out_ref, rows_ref):
    lo_x, beside_x, beneath_x = face_columns("sx", first_x_ref, below_x_ref)
    lo_y, beside_y, beneath_y = face_columns("sy", first_y_ref, below_y_ref)
    row = lax.broadcasted_iota(jnp.int32, lo_x[0].shape, 0)

    def put(base, value):
        rows_ref[pl.ds(base, NVEC), :] = value

    for b in range(NVEC):
        own = self_ref[pl.ds(b * NVEC, NVEC), :] + beside_x[b] + beside_y[b]
        put(PACKED + b * NVEC, jnp.where(row <= b, own, beneath_x[b]))
        put(XLO + b * NVEC, lo_x[b])
        put(YLO + b * NVEC, lo_y[b])
    for b in range(NVEC // 2):
        far = beneath_y[NVEC - 1 - b]
        put(TRIANGLE + b * NVEC, jnp.where(row > b, beneath_y[b], pltpu.roll(far, b, 0) if b else far))
    put(X_DIAG, diagonal_of(beneath_x, row))
    put(Y_DIAG, diagonal_of(beneath_y, row))
    put(RHS, self_ref[pl.ds(64, NVEC), :])
    put(RHS + NVEC, jnp.zeros_like(lo_x[0]))
    message = jnp.sum(rows_ref[...].T, axis=0, keepdims=True)
    out_ref[...] = jnp.broadcast_to(message[None], out_ref.shape)


def solve_kernel(got_ref, blocks_ref, coarse_ref, table_ref):
    count_y, window, words = got_ref.shape
    lanes = count_y * window
    index_x, index_y = lax.axis_index("sx"), lax.axis_index("sy")
    place = ROW + index_x % ROW - window_start(index_x, lax.axis_size("sx"))
    table_ref[...] = got_ref[...].reshape(lanes, words).T
    lane = lax.broadcasted_iota(jnp.int32, (1, lanes), 1)
    row = lax.broadcasted_iota(jnp.int32, (NVEC, lanes), 0)
    has_x = lane % window < window - 1
    has_y = lane < lanes - window

    def columns(base, count=NVEC):
        return [table_ref[pl.ds(base + b * NVEC, NVEC), :] for b in range(count)]

    def from_x(value):
        return jnp.where(has_x, pltpu.roll(value, lanes - 1, 1), 0.0)

    def from_y(value):
        return jnp.where(has_y, pltpu.roll(value, lanes - window, 1), 0.0)

    def product(matrix, vector):
        terms = [matrix[b] * vector[b : b + 1] for b in range(NVEC)]
        while len(terms) > 1:
            terms = [terms[i] + terms[i + 1] for i in range(0, len(terms), 2)]
        return terms[0]

    def mirrored(lower, upper, diagonal):
        return [
            jnp.where(row > b, lower[b], jnp.where(row < b, upper[b], diagonal)) for b in range(NVEC)
        ]

    packed = columns(PACKED)
    packed_t = transposed(packed)
    x_diag, y_diag = columns(X_DIAG, 2)
    beneath_x = mirrored(packed, packed_t, x_diag)
    lower = columns(TRIANGLE, NVEC // 2)
    lower = lower + [pltpu.roll(lower[c], NVEC - c, 0) if c else lower[c] for c in (3, 2, 1, 0)]
    beneath_y = mirrored(lower, transposed(lower), y_diag)
    own = [
        jnp.where(row <= b, packed[b], packed_t[b]) + from_x(beneath_x[b]) + from_y(beneath_y[b])
        for b in range(NVEC)
    ]
    inverse = list(own)
    for k in range(NVEC):
        pivot = 1.0 / inverse[k][k : k + 1]
        at_k = row == k
        column = inverse[k]
        for j in range(NVEC):
            if j != k:
                scaled = inverse[j][k : k + 1] * pivot
                inverse[j] = jnp.where(at_k, scaled, inverse[j] - column * scaled)
        inverse[k] = jnp.where(at_k, pivot, -column * pivot)

    right = table_ref[pl.ds(RHS, NVEC), :]
    xlo, ylo = columns(XLO), columns(YLO)
    xlo_t, ylo_t = transposed(xlo), transposed(ylo)
    coarse = OMEGA * product(inverse, right)
    for _ in range(ITERS - 1):
        remainder = right - product(own, coarse)
        remainder = remainder - product(xlo, pltpu.roll(coarse, 1, 1)) - from_x(product(xlo_t, coarse))
        remainder = remainder - product(ylo, pltpu.roll(coarse, window, 1)) - from_y(product(ylo_t, coarse))
        coarse = coarse + OMEGA * product(inverse, remainder)

    here = (lane == index_y * window + place).astype(jnp.float32)
    results = jnp.concatenate(
        own + xlo + [from_x(m) for m in xlo_t] + ylo + [from_y(m) for m in ylo_t] + [coarse], axis=0
    )
    flat = lax.dot_general(
        jnp.broadcast_to(here, (NVEC, lanes)),
        results,
        (((1,), (1,)), ((), ())),
        precision=HIGH,
        preferred_element_type=jnp.float32,
    )
    coarse_ref[...] = flat[:1, 320:328]
    entry = lax.broadcasted_iota(jnp.int32, (NVEC, 64), 1)
    matches = entry % NVEC == lax.broadcasted_iota(jnp.int32, (NVEC, 64), 0)
    spread = jnp.concatenate(
        [jnp.where(matches, flat[:, s * 64 : s * 64 + 64], 0.0) for s in range(5)], axis=0
    )
    select = (
        lax.broadcasted_iota(jnp.int32, (64, NVEC), 0) // NVEC == lax.broadcasted_iota(jnp.int32, (64, NVEC), 1)
    ).astype(jnp.float32)
    blocks_ref[...] = jnp.dot(spread, select, precision=HIGH, preferred_element_type=jnp.float32).reshape(5, 8, 8)


def window_start(index, count):
    chip_row = index // ROW
    low = jnp.where(chip_row > 0, 0, ROW)
    high = jnp.where(chip_row < count // ROW - 1, 3 * ROW, 2 * ROW) - WINDOW
    return jnp.clip(ROW + index % ROW - WINDOW // 2, low, high)


def window_kernel(lower_ref, line_ref, upper_ref, out_ref, rows_ref, near_ref):
    start = window_start(lax.axis_index("sx"), lax.axis_size("sx"))
    for part, ref in enumerate((lower_ref, line_ref, upper_ref)):
        for i in range(ROW):
            rows_ref[pl.ds(part * ROW + i, 1), :] = ref[i]
    for i in range(WINDOW):
        near_ref[pl.ds(i, 1), :] = rows_ref[pl.ds(start + i, 1), :]
    out_ref[...] = jnp.broadcast_to(near_ref[...][None], out_ref.shape)


def shape(*dims):
    return jax.ShapeDtypeStruct(dims, jnp.float32)


def per_device(strain_rate, deflation, residual):
    count_x, count_y = lax.axis_size("sx"), lax.axis_size("sy")
    last_x = jnp.concatenate([deflation[:, -1], strain_rate[None, -1]], 0)
    last_y = jnp.concatenate([deflation[:, :, -1], strain_rate[None, :, -1]], 0)
    below_x = lax.ppermute(last_x, "sx", [(i, i + 1) for i in range(count_x - 1)])
    below_y = lax.ppermute(last_y, "sy", [(i, i + 1) for i in range(count_y - 1)])
    first_x = jnp.concatenate([deflation[:, 0], strain_rate[None, 0]], 0)
    first_y = jnp.concatenate([deflation[:, :, 0], strain_rate[None, :, 0]], 0)
    cz = strain_rate.shape[-1]
    own_rows = pl.pallas_call(
        self_kernel,
        out_shape=shape(72, cz),
        in_specs=[
            pl.BlockSpec(memory_space=pltpu.VMEM),
            pl.BlockSpec(memory_space=pltpu.HBM),
            pl.BlockSpec(memory_space=pltpu.VMEM),
        ],
        scratch_shapes=[
            pltpu.VMEM(deflation.shape, jnp.float32),
            pltpu.VMEM(strain_rate.shape, jnp.float32),
            pltpu.VMEM((64, 8, cz), jnp.float32),
            pltpu.VMEM((NVEC, 8, cz), jnp.float32),
            pltpu.SemaphoreType.DMA((CHUNKS,)),
        ],
        compiler_params=pltpu.CompilerParams(vmem_limit_bytes=60 * 1024 * 1024),
        cost_estimate=pl.CostEstimate(flops=10000000, bytes_accessed=1400000, transcendentals=0),
        name="own_block",
    )(strain_rate, deflation, residual)
    messages = pl.pallas_call(
        face_kernel,
        out_shape=shape(ROW, 1, WORDS),
        scratch_shapes=[pltpu.VMEM((WORDS, cz), jnp.float32)],
        compiler_params=PARAMS,
        name="face_blocks",
    )(own_rows, first_x, first_y, below_x, below_y)
    rows = [[ROW * g + i for i in range(ROW)] for g in range(count_x // ROW)]
    line = lax.all_to_all(messages, "sx", 0, 0, axis_index_groups=rows)
    lower = lax.ppermute(line, "sx", [(i, i + ROW) for i in range(count_x - ROW)])
    upper = lax.ppermute(line, "sx", [(i + ROW, i) for i in range(count_x - ROW)])
    near = pl.pallas_call(
        window_kernel,
        out_shape=shape(count_y, WINDOW, WORDS),
        scratch_shapes=[pltpu.VMEM((3 * ROW, WORDS), jnp.float32), pltpu.VMEM((WINDOW, WORDS), jnp.float32)],
        compiler_params=PARAMS,
        name="window",
    )(lower, line, upper)
    got = lax.all_to_all(near, "sy", 0, 0)
    blocks, coarse = pl.pallas_call(
        solve_kernel,
        out_shape=(shape(5, NVEC, NVEC), shape(1, NVEC)),
        scratch_shapes=[pltpu.VMEM((WORDS, count_y * WINDOW), jnp.float32)],
        compiler_params=PARAMS,
        name="coarse_sweeps",
    )(got)
    return (blocks.reshape(1, 1, 5, NVEC, NVEC), coarse.reshape(1, 1, NVEC))


def solution(mesh):
    placed = (P("sx", "sy", None), P(None, "sx", "sy", None), P("sx", "sy", None))
    return jax.shard_map(
        per_device,
        mesh=mesh,
        in_specs=placed,
        out_specs=(P("sx", "sy", None, None, None), P("sx", "sy", None)),
        check_vma=False,
    )
```

```python
import jax
import jax.numpy as jnp
from jax import lax
from jax.experimental import pallas as pl
from jax.experimental.pallas import tpu as pltpu
from jax.sharding import PartitionSpec as P

NVEC = 8
ITERS = 6
SIGMA = 0.05
OMEGA = 0.6
HIGH = lax.Precision.HIGHEST

PACKED, TRIANGLE, X_DIAG, Y_DIAG, XLO, YLO, RHS, WORDS = (0, 64, 96, 104, 112, 176, 240, 256)
WINDOW = 16
ROW = 8
PARAMS = pltpu.CompilerParams(vmem_limit_bytes=32 * 1024 * 1024)


def viscosity(rate):
    return lax.rsqrt(rate) + 0.5 * (1.0 - jnp.exp(-10.0 * rate)) / rate


def fold(tiles):
    row = lax.broadcasted_iota(jnp.int32, tiles[0].shape, 0)
    for half in (4, 2, 1):
        low = (row & half) == 0
        count = len(tiles) // 2
        tiles = [
            jnp.where(
                low,
                tiles[i] + pltpu.roll(tiles[i], 8 - half, 0),
                tiles[i + count] + pltpu.roll(tiles[i + count], half, 0),
            )
            for i in range(count)
        ]
    return tiles[0]


def halves(x):
    return x[:8] + x[8:]


def pack_kernel(rate_ref, vec_ref, last_x_ref, last_y_ref, first_x_ref, first_y_ref):
    cx, cy, _ = rate_ref.shape
    for a in range(NVEC):
        last_x_ref[a] = vec_ref[a, cx - 1]
        first_x_ref[a] = vec_ref[a, 0]
        last_y_ref[a] = vec_ref[a, :, cy - 1, :]
        first_y_ref[a] = vec_ref[a, :, 0, :]
    last_x_ref[NVEC] = rate_ref[cx - 1]
    first_x_ref[NVEC] = rate_ref[0]
    last_y_ref[NVEC] = rate_ref[:, cy - 1, :]
    first_y_ref[NVEC] = rate_ref[:, 0, :]


def self_kernel(rate_ref, vec_ref, res_ref, out_ref, visc_ref, acc_ref, rhs_ref):
    at_top_x = lax.axis_index("sx") == lax.axis_size("sx") - 1
    at_top_y = lax.axis_index("sy") == lax.axis_size("sy") - 1
    visc_ref[...] = viscosity(rate_ref[...])
    acc_ref[...] = jnp.zeros_like(acc_ref)
    rhs_ref[...] = jnp.zeros_like(rhs_ref)
    cx, cy, cz = rate_ref.shape
    row = lax.broadcasted_iota(jnp.int32, (cy, cz), 0)
    lane = lax.broadcasted_iota(jnp.int32, (cy, cz), 1)
    top_x = jnp.where(at_top_x, 1.0, 0.5)
    top_y = jnp.where(at_top_y, 1.0, 0.5)

    @pl.loop(0, cx)
    def _(i):
        visc = visc_ref[i]
        after = visc_ref[jnp.minimum(i + 1, cx - 1)]
        before = visc_ref[jnp.maximum(i - 1, 0)]
        inner = i < cx - 1
        face_x = jnp.where(inner, 0.5 * (visc + after), 0.0)
        high_x = jnp.where(inner, face_x, top_x * visc)
        low_x = jnp.where(i > 0, 0.5 * (visc + before), 0.5 * visc)
        mean_y = 0.5 * (visc + pltpu.roll(visc, cy - 1, 0))
        face_y = jnp.where(row < cy - 1, mean_y, 0.0)
        high_y = jnp.where(row < cy - 1, mean_y, top_y * visc)
        low_y = jnp.where(row > 0, pltpu.roll(mean_y, 1, 0), 0.5 * visc)
        mean_z = 0.5 * (visc + pltpu.roll(visc, cz - 1, 1))
        face_z = jnp.where(lane < cz - 1, mean_z, 0.0)
        high_z = jnp.where(lane < cz - 1, mean_z, visc)
        low_z = jnp.where(lane > 0, pltpu.roll(mean_z, 1, 1), visc)
        weight = 0.5 * (SIGMA + (low_x + high_x) + (low_y + high_y) + (low_z + high_z))
        res = res_ref[i]
        following = jnp.minimum(i + 1, cx - 1)
        vectors = [vec_ref[a, i] for a in range(NVEC)]
        for a in range(NVEC):
            rhs_ref[a] += halves(vectors[a] * res)
        for b in range(NVEC):
            v = vectors[b]
            image = (
                weight * v
                - face_x * vec_ref[b, following]
                - face_y * pltpu.roll(v, cy - 1, 0)
                - face_z * pltpu.roll(v, cz - 1, 1)
            )
            for a in range(NVEC):
                acc_ref[b * NVEC + a] += halves(vectors[a] * image)

    for b in range(NVEC):
        out_ref[pl.ds(b * NVEC, NVEC), :] = fold(
            [acc_ref[b * NVEC + a] + acc_ref[a * NVEC + b] for a in range(NVEC)]
        )
    out_ref[pl.ds(NVEC * NVEC, NVEC), :] = fold([rhs_ref[a] for a in range(NVEC)])


def transposed(tiles):
    row = lax.broadcasted_iota(jnp.int32, tiles[0].shape, 0)
    tiles = list(tiles)
    for half in (4, 2, 1):
        low = (row & half) == 0
        for i in range(NVEC):
            if not i & half:
                p, q = tiles[i], tiles[i + half]
                tiles[i] = jnp.where(low, p, pltpu.roll(q, half, 0))
                tiles[i + half] = jnp.where(low, pltpu.roll(p, NVEC - half, 0), q)
    return tiles


def face_columns(axis, own, below):
    inner = lax.axis_index(axis) > 0
    visc = viscosity(own[NVEC])
    visc_below = viscosity(jnp.where(inner, below[NVEC], 1.0))
    coupling = jnp.where(inner, -0.5 * (visc + visc_below), 0.0)
    beside = 0.5 * jnp.where(inner, visc_below, visc)
    shared = jnp.where(inner, 0.5 * visc, 0.0)
    first = [own[a] for a in range(NVEC)]
    last = [below[a] for a in range(NVEC)]

    def gram(left, right, weight):
        columns = []
        for b in range(NVEC):
            scaled = weight * right[b]
            columns.append(fold([halves(left[a] * scaled) for a in range(NVEC)]))
        return columns

    return gram(first, last, coupling), gram(first, first, beside), gram(last, last, shared)


def diagonal_of(columns, row):
    result = columns[0]
    for b in range(1, NVEC):
        result = jnp.where(row == b, columns[b], result)
    return result


def face_kernel(self_ref, first_x_ref, first_y_ref, below_x_ref, below_y_ref, out_ref, rows_ref):
    lo_x, beside_x, beneath_x = face_columns("sx", first_x_ref, below_x_ref)
    lo_y, beside_y, beneath_y = face_columns("sy", first_y_ref, below_y_ref)
    row = lax.broadcasted_iota(jnp.int32, lo_x[0].shape, 0)

    def put(base, value):
        rows_ref[pl.ds(base, NVEC), :] = value

    for b in range(NVEC):
        own = self_ref[pl.ds(b * NVEC, NVEC), :] + beside_x[b] + beside_y[b]
        put(PACKED + b * NVEC, jnp.where(row <= b, own, beneath_x[b]))
        put(XLO + b * NVEC, lo_x[b])
        put(YLO + b * NVEC, lo_y[b])
    for b in range(NVEC // 2):
        far = beneath_y[NVEC - 1 - b]
        put(TRIANGLE + b * NVEC, jnp.where(row > b, beneath_y[b], pltpu.roll(far, b, 0) if b else far))
    put(X_DIAG, diagonal_of(beneath_x, row))
    put(Y_DIAG, diagonal_of(beneath_y, row))
    put(RHS, self_ref[pl.ds(64, NVEC), :])
    put(RHS + NVEC, jnp.zeros_like(lo_x[0]))
    message = jnp.sum(rows_ref[...].T, axis=0, keepdims=True)
    out_ref[...] = jnp.broadcast_to(message[None], out_ref.shape)


def solve_kernel(got_ref, blocks_ref, coarse_ref, table_ref):
    count_y, window, words = got_ref.shape
    lanes = count_y * window
    index_x, index_y = lax.axis_index("sx"), lax.axis_index("sy")
    place = ROW + index_x % ROW - window_start(index_x, lax.axis_size("sx"))
    table_ref[...] = got_ref[...].reshape(lanes, words).T
    lane = lax.broadcasted_iota(jnp.int32, (1, lanes), 1)
    row = lax.broadcasted_iota(jnp.int32, (NVEC, lanes), 0)
    has_x = lane % window < window - 1
    has_y = lane < lanes - window

    def columns(base, count=NVEC):
        return [table_ref[pl.ds(base + b * NVEC, NVEC), :] for b in range(count)]

    def from_x(value):
        return jnp.where(has_x, pltpu.roll(value, lanes - 1, 1), 0.0)

    def from_y(value):
        return jnp.where(has_y, pltpu.roll(value, lanes - window, 1), 0.0)

    def product(matrix, vector):
        terms = [matrix[b] * vector[b : b + 1] for b in range(NVEC)]
        while len(terms) > 1:
            terms = [terms[i] + terms[i + 1] for i in range(0, len(terms), 2)]
        return terms[0]

    def mirrored(lower, upper, diagonal):
        return [
            jnp.where(row > b, lower[b], jnp.where(row < b, upper[b], diagonal)) for b in range(NVEC)
        ]

    packed = columns(PACKED)
    packed_t = transposed(packed)
    x_diag, y_diag = columns(X_DIAG, 2)
    beneath_x = mirrored(packed, packed_t, x_diag)
    lower = columns(TRIANGLE, NVEC // 2)
    lower = lower + [pltpu.roll(lower[c], NVEC - c, 0) if c else lower[c] for c in (3, 2, 1, 0)]
    beneath_y = mirrored(lower, transposed(lower), y_diag)
    own = [
        jnp.where(row <= b, packed[b], packed_t[b]) + from_x(beneath_x[b]) + from_y(beneath_y[b])
        for b in range(NVEC)
    ]
    inverse = list(own)
    for k in range(NVEC):
        pivot = 1.0 / inverse[k][k : k + 1]
        at_k = row == k
        column = inverse[k]
        for j in range(NVEC):
            if j != k:
                scaled = inverse[j][k : k + 1] * pivot
                inverse[j] = jnp.where(at_k, scaled, inverse[j] - column * scaled)
        inverse[k] = jnp.where(at_k, pivot, -column * pivot)

    right = table_ref[pl.ds(RHS, NVEC), :]
    xlo, ylo = columns(XLO), columns(YLO)
    xlo_t, ylo_t = transposed(xlo), transposed(ylo)
    coarse = OMEGA * product(inverse, right)
    for _ in range(ITERS - 1):
        remainder = right - product(own, coarse)
        remainder = remainder - product(xlo, pltpu.roll(coarse, 1, 1)) - from_x(product(xlo_t, coarse))
        remainder = remainder - product(ylo, pltpu.roll(coarse, window, 1)) - from_y(product(ylo_t, coarse))
        coarse = coarse + OMEGA * product(inverse, remainder)

    here = (lane == index_y * window + place).astype(jnp.float32)
    results = jnp.concatenate(
        own + xlo + [from_x(m) for m in xlo_t] + ylo + [from_y(m) for m in ylo_t] + [coarse], axis=0
    )
    flat = lax.dot_general(
        jnp.broadcast_to(here, (NVEC, lanes)),
        results,
        (((1,), (1,)), ((), ())),
        precision=HIGH,
        preferred_element_type=jnp.float32,
    )
    coarse_ref[...] = flat[:1, 320:328]
    entry = lax.broadcasted_iota(jnp.int32, (NVEC, 64), 1)
    matches = entry % NVEC == lax.broadcasted_iota(jnp.int32, (NVEC, 64), 0)
    spread = jnp.concatenate(
        [jnp.where(matches, flat[:, s * 64 : s * 64 + 64], 0.0) for s in range(5)], axis=0
    )
    select = (
        lax.broadcasted_iota(jnp.int32, (64, NVEC), 0) // NVEC == lax.broadcasted_iota(jnp.int32, (64, NVEC), 1)
    ).astype(jnp.float32)
    blocks_ref[...] = jnp.dot(spread, select, precision=HIGH, preferred_element_type=jnp.float32).reshape(5, 8, 8)


def window_start(index, count):
    chip_row = index // ROW
    low = jnp.where(chip_row > 0, 0, ROW)
    high = jnp.where(chip_row < count // ROW - 1, 3 * ROW, 2 * ROW) - WINDOW
    return jnp.clip(ROW + index % ROW - WINDOW // 2, low, high)


def window_kernel(lower_ref, line_ref, upper_ref, out_ref, rows_ref, near_ref):
    start = window_start(lax.axis_index("sx"), lax.axis_size("sx"))
    for part, ref in enumerate((lower_ref, line_ref, upper_ref)):
        for i in range(ROW):
            rows_ref[pl.ds(part * ROW + i, 1), :] = ref[i]
    for i in range(WINDOW):
        near_ref[pl.ds(i, 1), :] = rows_ref[pl.ds(start + i, 1), :]
    out_ref[...] = jnp.broadcast_to(near_ref[...][None], out_ref.shape)


def shape(*dims):
    return jax.ShapeDtypeStruct(dims, jnp.float32)


def per_device(strain_rate, deflation, residual):
    count_x, count_y = lax.axis_size("sx"), lax.axis_size("sy")
    cz = strain_rate.shape[-1]
    last_x, last_y, first_x, first_y = pl.pallas_call(
        pack_kernel,
        out_shape=(shape(NVEC + 1, *strain_rate.shape[1:]), shape(NVEC + 1, strain_rate.shape[0], cz)) * 2,
        compiler_params=PARAMS,
        name="faces",
    )(strain_rate, deflation)
    below_x = lax.ppermute(last_x, "sx", [(i, i + 1) for i in range(count_x - 1)])
    below_y = lax.ppermute(last_y, "sy", [(i, i + 1) for i in range(count_y - 1)])
    own_rows = pl.pallas_call(
        self_kernel,
        out_shape=shape(72, cz),
        scratch_shapes=[
            pltpu.VMEM(strain_rate.shape, jnp.float32),
            pltpu.VMEM((64, 8, cz), jnp.float32),
            pltpu.VMEM((NVEC, 8, cz), jnp.float32),
        ],
        compiler_params=PARAMS,
        cost_estimate=pl.CostEstimate(flops=10000000, bytes_accessed=1400000, transcendentals=0),
        name="own_block",
    )(strain_rate, deflation, residual)
    messages = pl.pallas_call(
        face_kernel,
        out_shape=shape(ROW, 1, WORDS),
        scratch_shapes=[pltpu.VMEM((WORDS, cz), jnp.float32)],
        compiler_params=PARAMS,
        name="face_blocks",
    )(own_rows, first_x, first_y, below_x, below_y)
    rows = [[ROW * g + i for i in range(ROW)] for g in range(count_x // ROW)]
    line = lax.all_to_all(messages, "sx", 0, 0, axis_index_groups=rows)
    lower = lax.ppermute(line, "sx", [(i, i + ROW) for i in range(count_x - ROW)])
    upper = lax.ppermute(line, "sx", [(i + ROW, i) for i in range(count_x - ROW)])
    near = pl.pallas_call(
        window_kernel,
        out_shape=shape(count_y, WINDOW, WORDS),
        scratch_shapes=[pltpu.VMEM((3 * ROW, WORDS), jnp.float32), pltpu.VMEM((WINDOW, WORDS), jnp.float32)],
        compiler_params=PARAMS,
        name="window",
    )(lower, line, upper)
    got = lax.all_to_all(near, "sy", 0, 0)
    blocks, coarse = pl.pallas_call(
        solve_kernel,
        out_shape=(shape(5, NVEC, NVEC), shape(1, NVEC)),
        scratch_shapes=[pltpu.VMEM((WORDS, count_y * WINDOW), jnp.float32)],
        compiler_params=PARAMS,
        name="coarse_sweeps",
    )(got)
    return (blocks.reshape(1, 1, 5, NVEC, NVEC), coarse.reshape(1, 1, NVEC))


def solution(mesh):
    placed = (P("sx", "sy", None), P(None, "sx", "sy", None), P("sx", "sy", None))
    return jax.shard_map(
        per_device,
        mesh=mesh,
        in_specs=placed,
        out_specs=(P("sx", "sy", None, None, None), P("sx", "sy", None)),
        check_vma=False,
    )
```

```python
import jax
import jax.numpy as jnp
from jax import lax
from jax.experimental import pallas as pl
from jax.experimental.pallas import tpu as pltpu
from jax.sharding import PartitionSpec as P

NVEC = 8
ITERS = 6
SIGMA = 0.05
OMEGA = 0.6
HIGH = lax.Precision.HIGHEST

PACKED, TRIANGLE, X_DIAG, Y_DIAG, XLO, YLO, RHS, WORDS = (0, 64, 96, 104, 112, 176, 240, 256)
WINDOW = 16
ROW = 8
PARAMS = pltpu.CompilerParams(vmem_limit_bytes=32 * 1024 * 1024)


def viscosity(rate):
    return lax.rsqrt(rate) + 0.5 * (1.0 - jnp.exp(-10.0 * rate)) / rate


def fold(tiles):
    row = lax.broadcasted_iota(jnp.int32, tiles[0].shape, 0)
    for half in (4, 2, 1):
        low = (row & half) == 0
        count = len(tiles) // 2
        tiles = [
            jnp.where(
                low,
                tiles[i] + pltpu.roll(tiles[i], 8 - half, 0),
                tiles[i + count] + pltpu.roll(tiles[i + count], half, 0),
            )
            for i in range(count)
        ]
    return tiles[0]


def halves(x):
    return x[:8] + x[8:]


def pack_kernel(visc_ref, vec_ref, last_x_ref, last_y_ref, first_x_ref, first_y_ref):
    cx, cy, _ = visc_ref.shape
    for a in range(NVEC):
        last_x_ref[a] = vec_ref[a, cx - 1]
        first_x_ref[a] = vec_ref[a, 0]
        last_y_ref[a] = vec_ref[a, :, cy - 1, :]
        first_y_ref[a] = vec_ref[a, :, 0, :]
    last_x_ref[NVEC] = visc_ref[cx - 1]
    first_x_ref[NVEC] = visc_ref[0]
    last_y_ref[NVEC] = visc_ref[:, cy - 1, :]
    first_y_ref[NVEC] = visc_ref[:, 0, :]


def self_kernel(visc_ref, vec_ref, res_ref, out_ref, acc_ref, rhs_ref):
    at_top_x = lax.axis_index("sx") == lax.axis_size("sx") - 1
    at_top_y = lax.axis_index("sy") == lax.axis_size("sy") - 1
    acc_ref[...] = jnp.zeros_like(acc_ref)
    rhs_ref[...] = jnp.zeros_like(rhs_ref)
    cx, cy, cz = visc_ref.shape
    row = lax.broadcasted_iota(jnp.int32, (cy, cz), 0)
    lane = lax.broadcasted_iota(jnp.int32, (cy, cz), 1)
    top_x = jnp.where(at_top_x, 1.0, 0.5)
    top_y = jnp.where(at_top_y, 1.0, 0.5)

    @pl.loop(0, cx)
    def _(i):
        visc = visc_ref[i]
        after = visc_ref[jnp.minimum(i + 1, cx - 1)]
        before = visc_ref[jnp.maximum(i - 1, 0)]
        inner = i < cx - 1
        face_x = jnp.where(inner, 0.5 * (visc + after), 0.0)
        high_x = jnp.where(inner, face_x, top_x * visc)
        low_x = jnp.where(i > 0, 0.5 * (visc + before), 0.5 * visc)
        mean_y = 0.5 * (visc + pltpu.roll(visc, cy - 1, 0))
        face_y = jnp.where(row < cy - 1, mean_y, 0.0)
        high_y = jnp.where(row < cy - 1, mean_y, top_y * visc)
        low_y = jnp.where(row > 0, pltpu.roll(mean_y, 1, 0), 0.5 * visc)
        mean_z = 0.5 * (visc + pltpu.roll(visc, cz - 1, 1))
        face_z = jnp.where(lane < cz - 1, mean_z, 0.0)
        high_z = jnp.where(lane < cz - 1, mean_z, visc)
        low_z = jnp.where(lane > 0, pltpu.roll(mean_z, 1, 1), visc)
        weight = 0.5 * (SIGMA + (low_x + high_x) + (low_y + high_y) + (low_z + high_z))
        res = res_ref[i]
        following = jnp.minimum(i + 1, cx - 1)
        vectors = [vec_ref[a, i] for a in range(NVEC)]
        for a in range(NVEC):
            rhs_ref[a] += halves(vectors[a] * res)
        for b in range(NVEC):
            v = vectors[b]
            image = (
                weight * v
                - face_x * vec_ref[b, following]
                - face_y * pltpu.roll(v, cy - 1, 0)
                - face_z * pltpu.roll(v, cz - 1, 1)
            )
            for a in range(NVEC):
                acc_ref[b * NVEC + a] += halves(vectors[a] * image)

    for b in range(NVEC):
        out_ref[pl.ds(b * NVEC, NVEC), :] = fold(
            [acc_ref[b * NVEC + a] + acc_ref[a * NVEC + b] for a in range(NVEC)]
        )
    out_ref[pl.ds(NVEC * NVEC, NVEC), :] = fold([rhs_ref[a] for a in range(NVEC)])


def transposed(tiles):
    row = lax.broadcasted_iota(jnp.int32, tiles[0].shape, 0)
    tiles = list(tiles)
    for half in (4, 2, 1):
        low = (row & half) == 0
        for i in range(NVEC):
            if not i & half:
                p, q = tiles[i], tiles[i + half]
                tiles[i] = jnp.where(low, p, pltpu.roll(q, half, 0))
                tiles[i + half] = jnp.where(low, pltpu.roll(p, NVEC - half, 0), q)
    return tiles


def face_columns(axis, own, below):
    inner = lax.axis_index(axis) > 0
    visc = own[NVEC]
    visc_below = below[NVEC]
    coupling = jnp.where(inner, -0.5 * (visc + visc_below), 0.0)
    beside = 0.5 * jnp.where(inner, visc_below, visc)
    shared = jnp.where(inner, 0.5 * visc, 0.0)
    first = [own[a] for a in range(NVEC)]
    last = [below[a] for a in range(NVEC)]

    def gram(left, right, weight):
        columns = []
        for b in range(NVEC):
            scaled = weight * right[b]
            columns.append(fold([halves(left[a] * scaled) for a in range(NVEC)]))
        return columns

    return gram(first, last, coupling), gram(first, first, beside), gram(last, last, shared)


def diagonal_of(columns, row):
    result = columns[0]
    for b in range(1, NVEC):
        result = jnp.where(row == b, columns[b], result)
    return result


def face_kernel(self_ref, first_x_ref, first_y_ref, below_x_ref, below_y_ref, out_ref, rows_ref):
    lo_x, beside_x, beneath_x = face_columns("sx", first_x_ref, below_x_ref)
    lo_y, beside_y, beneath_y = face_columns("sy", first_y_ref, below_y_ref)
    row = lax.broadcasted_iota(jnp.int32, lo_x[0].shape, 0)

    def put(base, value):
        rows_ref[pl.ds(base, NVEC), :] = value

    for b in range(NVEC):
        own = self_ref[pl.ds(b * NVEC, NVEC), :] + beside_x[b] + beside_y[b]
        put(PACKED + b * NVEC, jnp.where(row <= b, own, beneath_x[b]))
        put(XLO + b * NVEC, lo_x[b])
        put(YLO + b * NVEC, lo_y[b])
    for b in range(NVEC // 2):
        far = beneath_y[NVEC - 1 - b]
        put(TRIANGLE + b * NVEC, jnp.where(row > b, beneath_y[b], pltpu.roll(far, b, 0) if b else far))
    put(X_DIAG, diagonal_of(beneath_x, row))
    put(Y_DIAG, diagonal_of(beneath_y, row))
    put(RHS, self_ref[pl.ds(64, NVEC), :])
    put(RHS + NVEC, jnp.zeros_like(lo_x[0]))
    message = jnp.sum(rows_ref[...].T, axis=0, keepdims=True)
    out_ref[...] = jnp.broadcast_to(message[None], out_ref.shape)


def solve_kernel(got_ref, blocks_ref, coarse_ref, table_ref):
    count_y, window, words = got_ref.shape
    lanes = count_y * window
    index_x, index_y = lax.axis_index("sx"), lax.axis_index("sy")
    place = ROW + index_x % ROW - window_start(index_x, lax.axis_size("sx"))
    table_ref[...] = got_ref[...].reshape(lanes, words).T
    lane = lax.broadcasted_iota(jnp.int32, (1, lanes), 1)
    row = lax.broadcasted_iota(jnp.int32, (NVEC, lanes), 0)
    has_x = lane % window < window - 1
    has_y = lane < lanes - window

    def columns(base, count=NVEC):
        return [table_ref[pl.ds(base + b * NVEC, NVEC), :] for b in range(count)]

    def from_x(value):
        return jnp.where(has_x, pltpu.roll(value, lanes - 1, 1), 0.0)

    def from_y(value):
        return jnp.where(has_y, pltpu.roll(value, lanes - window, 1), 0.0)

    def product(matrix, vector):
        terms = [matrix[b] * vector[b : b + 1] for b in range(NVEC)]
        while len(terms) > 1:
            terms = [terms[i] + terms[i + 1] for i in range(0, len(terms), 2)]
        return terms[0]

    def mirrored(lower, upper, diagonal):
        return [
            jnp.where(row > b, lower[b], jnp.where(row < b, upper[b], diagonal)) for b in range(NVEC)
        ]

    packed = columns(PACKED)
    packed_t = transposed(packed)
    x_diag, y_diag = columns(X_DIAG, 2)
    beneath_x = mirrored(packed, packed_t, x_diag)
    lower = columns(TRIANGLE, NVEC // 2)
    lower = lower + [pltpu.roll(lower[c], NVEC - c, 0) if c else lower[c] for c in (3, 2, 1, 0)]
    beneath_y = mirrored(lower, transposed(lower), y_diag)
    own = [
        jnp.where(row <= b, packed[b], packed_t[b]) + from_x(beneath_x[b]) + from_y(beneath_y[b])
        for b in range(NVEC)
    ]
    inverse = list(own)
    for k in range(NVEC):
        pivot = 1.0 / inverse[k][k : k + 1]
        at_k = row == k
        column = inverse[k]
        for j in range(NVEC):
            if j != k:
                scaled = inverse[j][k : k + 1] * pivot
                inverse[j] = jnp.where(at_k, scaled, inverse[j] - column * scaled)
        inverse[k] = jnp.where(at_k, pivot, -column * pivot)

    right = table_ref[pl.ds(RHS, NVEC), :]
    xlo, ylo = columns(XLO), columns(YLO)
    xlo_t, ylo_t = transposed(xlo), transposed(ylo)
    coarse = OMEGA * product(inverse, right)
    for _ in range(ITERS - 1):
        remainder = right - product(own, coarse)
        remainder = remainder - product(xlo, pltpu.roll(coarse, 1, 1)) - from_x(product(xlo_t, coarse))
        remainder = remainder - product(ylo, pltpu.roll(coarse, window, 1)) - from_y(product(ylo_t, coarse))
        coarse = coarse + OMEGA * product(inverse, remainder)

    here = (lane == index_y * window + place).astype(jnp.float32)
    results = jnp.concatenate(
        own + xlo + [from_x(m) for m in xlo_t] + ylo + [from_y(m) for m in ylo_t] + [coarse], axis=0
    )
    flat = lax.dot_general(
        jnp.broadcast_to(here, (NVEC, lanes)),
        results,
        (((1,), (1,)), ((), ())),
        precision=HIGH,
        preferred_element_type=jnp.float32,
    )
    coarse_ref[...] = flat[:1, 320:328]
    entry = lax.broadcasted_iota(jnp.int32, (NVEC, 64), 1)
    matches = entry % NVEC == lax.broadcasted_iota(jnp.int32, (NVEC, 64), 0)
    spread = jnp.concatenate(
        [jnp.where(matches, flat[:, s * 64 : s * 64 + 64], 0.0) for s in range(5)], axis=0
    )
    select = (
        lax.broadcasted_iota(jnp.int32, (64, NVEC), 0) // NVEC == lax.broadcasted_iota(jnp.int32, (64, NVEC), 1)
    ).astype(jnp.float32)
    blocks_ref[...] = jnp.dot(spread, select, precision=HIGH, preferred_element_type=jnp.float32).reshape(5, 8, 8)


def window_start(index, count):
    chip_row = index // ROW
    low = jnp.where(chip_row > 0, 0, ROW)
    high = jnp.where(chip_row < count // ROW - 1, 3 * ROW, 2 * ROW) - WINDOW
    return jnp.clip(ROW + index % ROW - WINDOW // 2, low, high)


def window_kernel(lower_ref, line_ref, upper_ref, out_ref, rows_ref, near_ref):
    start = window_start(lax.axis_index("sx"), lax.axis_size("sx"))
    for part, ref in enumerate((lower_ref, line_ref, upper_ref)):
        for i in range(ROW):
            rows_ref[pl.ds(part * ROW + i, 1), :] = ref[i]
    for i in range(WINDOW):
        near_ref[pl.ds(i, 1), :] = rows_ref[pl.ds(start + i, 1), :]
    out_ref[...] = jnp.broadcast_to(near_ref[...][None], out_ref.shape)


def shape(*dims):
    return jax.ShapeDtypeStruct(dims, jnp.float32)


def per_device(strain_rate, deflation, residual):
    count_x, count_y = lax.axis_size("sx"), lax.axis_size("sy")
    cz = strain_rate.shape[-1]
    viscous = viscosity(strain_rate)
    last_x, last_y, first_x, first_y = pl.pallas_call(
        pack_kernel,
        out_shape=(shape(NVEC + 1, *strain_rate.shape[1:]), shape(NVEC + 1, strain_rate.shape[0], cz)) * 2,
        compiler_params=PARAMS,
        name="faces",
    )(viscous, deflation)
    below_x = lax.ppermute(last_x, "sx", [(i, i + 1) for i in range(count_x - 1)])
    below_y = lax.ppermute(last_y, "sy", [(i, i + 1) for i in range(count_y - 1)])
    own_rows = pl.pallas_call(
        self_kernel,
        out_shape=shape(72, cz),
        scratch_shapes=[
            pltpu.VMEM((64, 8, cz), jnp.float32),
            pltpu.VMEM((NVEC, 8, cz), jnp.float32),
        ],
        compiler_params=PARAMS,
        cost_estimate=pl.CostEstimate(flops=10000000, bytes_accessed=1400000, transcendentals=0),
        name="own_block",
    )(viscous, deflation, residual)
    messages = pl.pallas_call(
        face_kernel,
        out_shape=shape(ROW, 1, WORDS),
        scratch_shapes=[pltpu.VMEM((WORDS, cz), jnp.float32)],
        compiler_params=PARAMS,
        name="face_blocks",
    )(own_rows, first_x, first_y, below_x, below_y)
    rows = [[ROW * g + i for i in range(ROW)] for g in range(count_x // ROW)]
    line = lax.all_to_all(messages, "sx", 0, 0, axis_index_groups=rows)
    lower = lax.ppermute(line, "sx", [(i, i + ROW) for i in range(count_x - ROW)])
    upper = lax.ppermute(line, "sx", [(i + ROW, i) for i in range(count_x - ROW)])
    near = pl.pallas_call(
        window_kernel,
        out_shape=shape(count_y, WINDOW, WORDS),
        scratch_shapes=[pltpu.VMEM((3 * ROW, WORDS), jnp.float32), pltpu.VMEM((WINDOW, WORDS), jnp.float32)],
        compiler_params=PARAMS,
        name="window",
    )(lower, line, upper)
    got = lax.all_to_all(near, "sy", 0, 0)
    blocks, coarse = pl.pallas_call(
        solve_kernel,
        out_shape=(shape(5, NVEC, NVEC), shape(1, NVEC)),
        scratch_shapes=[pltpu.VMEM((WORDS, count_y * WINDOW), jnp.float32)],
        compiler_params=PARAMS,
        name="coarse_sweeps",
    )(got)
    return (blocks.reshape(1, 1, 5, NVEC, NVEC), coarse.reshape(1, 1, NVEC))


def solution(mesh):
    placed = (P("sx", "sy", None), P(None, "sx", "sy", None), P("sx", "sy", None))
    return jax.shard_map(
        per_device,
        mesh=mesh,
        in_specs=placed,
        out_specs=(P("sx", "sy", None, None, None), P("sx", "sy", None)),
        check_vma=False,
    )
```
